32 devices in a mesh: gx: 8 (over z, core), gy: 4 (over y, x).
Axes of the slice: x: 2, y: 2, z: 4, core: 2. Of those that a mesh axis runs over, the one named last changes fastest.
Arguments:
- adjoint_fields: float32 [6, 64, 128, 128], P(None, 'gx', 'gy'), may hold values from -6 to 6
- forward_e: bfloat16 [4, 3, 64, 128, 128], P(None, None, 'gx', 'gy'), may hold values from -6 to 6
- permittivity: float32 [64, 128, 128], P('gx', 'gy'), may hold values from 1 to 12
- design_mask: int32 [64, 128, 128], P('gx', 'gy'), may hold values 0 or 1
- band_offsets: int32 [9], replicated, may hold values from -16 to 16, as said below
- filter_taps: float32 [9], replicated, may hold values from 0.05 to 0.5
Outputs:
- filtered: float32 [64, 128, 128], P('gx', 'gy')
- adjoint_e: float32 [3, 64, 128, 128], P(None, 'gx', 'gy')
The draws below stay inside these ranges and needn't reach their ends.
Inputs may be any that keep to these rules, and one draw needn't show every extreme that they name: `band_offsets`: the offsets are distinct; both -16 and 16 occur.
All inputs are finite; a program needn't handle non-finite values. No bound on the sum of `design_mask` on one device may be relied on, other than what follows from the above.
Results may differ from the reference program's by a relative error of at most 0.0003.
Values sent between devices are 32-bit elements; how exact they have to be, the bound alone decides.
No kernel may reach another device: no remote copies, remote signals or barrier semaphores. Data moves between devices by JAX's collectives and lax.ppermute only.
A program may use at most 64 MiB of HBM per device.

```python
import math
import jax
import jax.numpy as jnp
from jax import lax

NZ = 128
ITERS = 4
BAND = 9
NX = 64
NY = 128
REACH = 16


def draw_band_offsets(key, part):
    inner = jax.random.permutation(key, 2 * REACH - 1)[:BAND - 2].astype(jnp.int32) - (REACH - 1)
    ends = jnp.array([-REACH, REACH], jnp.int32)
    return jnp.concatenate([ends, inner])


def plant(result, stream_key, low, high):
    extent = result.shape
    index_at = [jax.random.randint(jax.random.fold_in(stream_key, axis), (), 0, extent[axis]) for axis in range(len(extent))]
    result = result.at[tuple(index_at)].set(low)
    longest = extent.index(max(extent))
    index_at[longest] = (index_at[longest] + 1) % extent[longest]
    return result.at[tuple(index_at)].set(high)


def block_scale(own_key, dims, pieces, least, top_value):
    factor_of, own = 1.0, jax.random.fold_in(own_key, 6)
    for position, parts in pieces:
        steps = jnp.exp(jax.random.uniform(jax.random.fold_in(own, position), (parts,), jnp.float32, least / len(pieces), top_value / len(pieces)))
        factor_of = factor_of * jnp.repeat(steps, dims[position] // parts).reshape([-1 if axis == position else 1 for axis in range(len(dims))])
    return factor_of


def noise(own_key, dims, deviation, bound, pieces=(), kind=jnp.bfloat16):
    drawn = jax.random.normal(own_key, dims, jnp.float32) * deviation
    if len(pieces) > 0:
        drawn = block_scale(own_key, dims, pieces, -0.22, 0.18) * drawn
    return jnp.clip(drawn, min=-bound, max=bound).astype(kind)


def setup_inputs(seed: int = 0) -> dict:
    seeds = jax.random.split(jax.random.key(seed), 7)
    adjoint_fields = noise(seeds[0], (6, NX, NY, NZ), 1.0, 6.0, ((1, 8), (2, 4)), jnp.float32)
    forward_e = noise(seeds[1], (ITERS, 3, NX, NY, NZ), 1.0, 6.0, ((2, 8), (3, 4)))
    permittivity = jnp.clip(1.0 + 11.0 * jax.random.uniform(seeds[2], (NX, NY, NZ), jnp.float32) ** block_scale(seeds[2], (NX, NY, NZ), ((0, 8), (1, 4)), -0.2, 0.2), 1.0, 12.0)
    design_mask = plant((jax.random.randint(seeds[3], (NX, NY, NZ), 0, 4) < 3).astype(jnp.int32), jax.random.fold_in(seeds[3], 1), 0, 1)
    band_offsets = draw_band_offsets(jax.random.fold_in(seeds[6], 71), 0)
    filter_taps = jnp.clip(jnp.exp(jax.random.uniform(seeds[5], (BAND,), jnp.float32, math.log(0.05), math.log(0.5))), 0.05, 0.5)
    return {"adjoint_fields": adjoint_fields, "forward_e": forward_e, "permittivity": permittivity, "design_mask": design_mask, "band_offsets": band_offsets, "filter_taps": filter_taps}


courant = 0.5


def forward_diff(quantity, along):
    widths = [(0, 0)] * quantity.ndim
    widths[along] = (0, 1)
    padded = jnp.pad(quantity, widths)
    return lax.slice_in_dim(padded, 1, quantity.shape[along] + 1, axis=along) - quantity


def backward_diff(quantity, along):
    widths = [(0, 0)] * quantity.ndim
    widths[along] = (1, 0)
    padded = jnp.pad(quantity, widths)
    return quantity - lax.slice_in_dim(padded, 0, quantity.shape[along], axis=along)


def reference(adjoint_fields, forward_e, permittivity, design_mask, band_offsets, filter_taps):
    elec_x, elec_y, elec_z = adjoint_fields[0], adjoint_fields[1], adjoint_fields[2]
    magn_x, magn_y, magn_z = adjoint_fields[3], adjoint_fields[4], adjoint_fields[5]
    factor = courant / permittivity
    gradient = jnp.zeros(permittivity.shape, jnp.float32)
    for turn in range(ITERS):
        magn_x = magn_x - courant * (forward_diff(elec_z, 1) - forward_diff(elec_y, 2))
        magn_y = magn_y - courant * (forward_diff(elec_x, 2) - forward_diff(elec_z, 0))
        magn_z = magn_z - courant * (forward_diff(elec_y, 0) - forward_diff(elec_x, 1))
        elec_x = elec_x + factor * (backward_diff(magn_z, 1) - backward_diff(magn_y, 2))
        elec_y = elec_y + factor * (backward_diff(magn_x, 2) - backward_diff(magn_z, 0))
        elec_z = elec_z + factor * (backward_diff(magn_y, 0) - backward_diff(magn_x, 1))
        stored = forward_e[turn].astype(jnp.float32)
        gradient = gradient + (stored[0] * elec_x + stored[1] * elec_y + stored[2] * elec_z)
    masked = gradient * design_mask.astype(jnp.float32)
    total = masked.shape[0]
    padded = jnp.pad(masked, ((REACH, REACH), (0, 0), (0, 0)))
    filtered = jnp.zeros(masked.shape, jnp.float32)
    for index in range(BAND):
        start = (REACH + band_offsets[index]).astype(jnp.int32)
        filtered = filtered + filter_taps[index] * lax.dynamic_slice_in_dim(padded, start, total, 0)
    return filtered, jnp.stack([elec_x, elec_y, elec_z])
```

```python
import functools
import jax
import jax.numpy as jnp
from jax import lax
from jax.experimental import pallas as pl
from jax.experimental.pallas import tpu as pltpu
from jax.sharding import PartitionSpec as P

ITERS = 4
COURANT = 0.5
BOTH = ("gx", "gy")
SUB = 8


def swaps(count_x, count_y, partner, idle):
    pairs = []
    for x in range(count_x):
        for y in range(count_y):
            to = partner(x, y)
            if to is None:
                to = idle(x, y)
            pairs.append((x * count_y + y, to[0] * count_y + to[1]))
    assert sorted(b for _, b in pairs) == sorted(a for a, _ in pairs)
    return pairs


class Routes:
    def __init__(self, count_x, count_y):
        self.count_x, self.count_y = count_x, count_y
        half = max(count_y // 2, 1)

        def outward_x(x):
            to = x + 1 if x % 2 else x - 1
            return to if 0 <= to < count_x else None

        def side_b(y):
            to = y + 1 if y % 2 else y - 1
            return to if 0 <= to < count_y else None

        def far_y(x, y):
            return (x, (y + half) % count_y)

        def out_partner(x, y):
            return None if outward_x(x) is None else (outward_x(x), y)

        def b_partner(x, y):
            return None if side_b(y) is None else (x, side_b(y))

        def diag_a(x, y):
            return None if outward_x(x) is None else (outward_x(x), y ^ 1)

        def diag_b(x, y):
            if outward_x(x) is None:
                return None
            return (outward_x(x), y if side_b(y) is None else side_b(y))

        def pair_b(x, y):
            to = (x // 2 + (1 if (x // 2) % 2 else -1)) * 2 + x % 2
            return (to, y) if 0 <= to < count_x else None

        make = functools.partial(swaps, count_x, count_y)
        core = lambda x, y: (x ^ 1, y)
        self.core = make(core, None)
        self.out_x = make(out_partner, far_y)
        self.side_a = make(lambda x, y: (x, y ^ 1), None)
        self.side_b = make(b_partner, core)
        self.diag_a = make(diag_a, lambda x, y: (x, y ^ 1))
        self.diag_b = make(diag_b, far_y)
        self.pair_a = make(lambda x, y: (x ^ 2, y), None)
        self.pair_b = make(pair_b, core)


def depths(margin):
    return (margin, margin, margin, margin - 1, margin, margin, margin - 1)


def pack(margin, fields, perm, out_x, in_x, side_a, side_b, diag_a, diag_b):
    width, rows = perm.shape[0], perm.shape[1]
    core = lax.rem(lax.axis_index("gx"), 2)
    odd = lax.rem(lax.axis_index("gy"), 2)
    low = lax.broadcasted_iota(jnp.int32, (SUB, perm.shape[2]), 0) < SUB // 2

    def plane_of(k, x, where):
        return fields[k, x, where] if k < 6 else perm[x, where]

    at = 0
    for k, depth in enumerate(depths(margin)):
        for j in range(depth):
            out_x[at + j] = plane_of(k, core * (width - depth) + j, slice(None))
            in_x[at + j] = plane_of(k, (1 - core) * (width - depth) + j, slice(None))
        at += depth

    def edge(k, x, x2, upper):
        where = pl.ds(pl.multiple_of(upper * (rows - SUB), SUB), SUB)
        first, second = plane_of(k, x, where), plane_of(k, x2, where)
        up = upper == 1
        first = jnp.where(up, pltpu.roll(first, SUB // 2, 0), first)
        second = jnp.where(up, second, pltpu.roll(second, SUB // 2, 0))
        return jnp.where(low, first, second)

    for k in range(7):
        for j in range(width // 2):
            side_a[k, j] = edge(k, j, j + width // 2, 1 - odd)
            side_b[k, j] = edge(k, j, j + width // 2, odd)
        for j in range(margin // 2):
            x = core * (width - margin) + j
            diag_a[k, j] = edge(k, x, x + margin // 2, 1 - odd)
            diag_b[k, j] = edge(k, x, x + margin // 2, odd)


def steps(margin, count_x, count_y, fields, perm, forward, mask, out_x, in_x, side_a, side_b, diag_a, diag_b, core_a, core_b,
          masked, final, ext, factor, own_sem, forward_buf, forward_sem):
    width, rows, lanes = perm.shape
    at_x, at_y = lax.axis_index("gx"), lax.axis_index("gy")
    core, odd = lax.rem(at_x, 2), lax.rem(at_y, 2)
    half = SUB // 2
    own = pltpu.make_async_copy(fields, ext.at[:, pl.ds(margin, width), pl.ds(0, rows)], own_sem)
    own.start()
    load_forward = pltpu.make_async_copy(forward, forward_buf, forward_sem)
    load_forward.start()

    scale = COURANT * COURANT
    low = lax.broadcasted_iota(jnp.int32, (SUB, lanes), 0) < half
    has_out = jnp.where(core == 0, at_x > 0, at_x < count_x - 1)
    has_after, has_before = at_y < count_y - 1, at_y > 0
    out_at = core * (width + margin)
    in_at = (1 - core) * (width + margin)

    def put(k, x, where, value, valid):
        if k < 6:
            ext[k, x, where] = value if valid is None else jnp.where(valid, value, 0.0)
        else:
            value = scale / value
            factor[x, where] = value if valid is None else jnp.where(valid, value, 0.0)

    body, tail = pl.ds(0, rows), pl.ds(rows, SUB)
    for x in range(width):
        factor[margin + x, body] = scale / perm[x]
    at = 0
    for k, depth in enumerate(depths(margin)):
        for j in range(depth):
            put(k, out_at + (1 - core) * (margin - depth) + j, body, out_x[at + j], has_out)
            put(k, in_at + core * (margin - depth) + j, body, in_x[at + j], None)
        at += depth

    def tail_tile(first, second, upper):
        after = jnp.where(odd == 0, first, second)
        before = jnp.where(odd == 0, second, first)
        if isinstance(upper, int):
            after = pltpu.roll(after, half, 0) if upper else after
            before = before if upper else pltpu.roll(before, half, 0)
        else:
            after = jnp.where(upper == 1, pltpu.roll(after, half, 0), after)
            before = jnp.where(upper == 1, before, pltpu.roll(before, half, 0))
        return jnp.where(low, after, before)

    valid_tail = jnp.where(low, jnp.where(has_after, 1, 0), jnp.where(has_before, 1, 0)) > 0
    valid_corner = valid_tail & jnp.broadcast_to(has_out, (SUB, lanes))
    for k in range(7):
        for j in range(width // 2):
            put(k, margin + j, tail, tail_tile(side_a[k, j], side_b[k, j], 0), valid_tail)
            put(k, margin + j + width // 2, tail, tail_tile(side_a[k, j], side_b[k, j], 1), valid_tail)
        for j in range(margin // 2):
            put(k, out_at + j, tail, tail_tile(diag_a[k, j], diag_b[k, j], 0), valid_corner)
            put(k, out_at + j + margin // 2, tail, tail_tile(diag_a[k, j], diag_b[k, j], 1), valid_corner)
        for j in range(margin):
            tile = core * (width // 2 - margin) + j
            put(k, in_at + j, tail, tail_tile(core_a[k, tile], core_b[k, tile], core), valid_tail)

    lane = lax.broadcasted_iota(jnp.int32, (rows + SUB, lanes), 1)
    first_lane, last_lane = lane == 0, lane == lanes - 1
    before_rows = jnp.where(low | jnp.broadcast_to(has_before, (SUB, lanes)), 1.0, 0.0)
    before_x = jnp.where(at_x > 0, 1.0, 0.0)

    def next_y(f):
        return pltpu.roll(f, rows + SUB - 1, 0)

    def last_y(f):
        return pltpu.roll(f, 1, 0)

    def next_z(f):
        return jnp.where(last_lane, 0.0, pltpu.roll(f, lanes - 1, 1))

    def last_z(f):
        return jnp.where(first_lane, 0.0, pltpu.roll(f, 1, 1))

    own.wait()
    load_forward.wait()
    for turn in range(margin):
        last = turn == margin - 1
        held_y = held_z = None
        for i in range(turn, width + 2 * margin - 1 - turn):
            ex, ey, ez = ext[0, i], ext[1, i], ext[2, i]
            ey_x, ez_x = ext[1, i + 1], ext[2, i + 1]
            hx, hy, hz = ext[3, i], ext[4, i], ext[5, i]
            if turn == 0:
                hx, hy, hz = hx * (1 / COURANT), hy * (1 / COURANT), hz * (1 / COURANT)
            hx = hx - ((next_y(ez) - ez) - (next_z(ey) - ey))
            hy = hy - ((next_z(ex) - ex) - (ez_x - ez))
            hz = hz - ((ey_x - ey) - (next_y(ex) - ex))

            def clear(h):
                h = jnp.concatenate([h[:rows], h[rows:] * before_rows], 0)
                return h * before_x if i < margin else h

            hx, hy, hz = clear(hx), clear(hy), clear(hz)
            if not last:
                ext[3, i], ext[4, i], ext[5, i] = hx, hy, hz
            if i > turn:
                c = factor[i]
                ex = ex + c * ((hz - last_y(hz)) - (hy - last_z(hy)))
                ey = ey + c * ((hx - last_z(hx)) - (hz - held_z))
                ez = ez + c * ((hy - held_y) - (hx - last_y(hx)))
                if not last:
                    ext[0, i], ext[1, i], ext[2, i] = ex, ey, ez
                if margin <= i < margin + width:
                    x = i - margin
                    own_e = (ex[:rows], ey[:rows], ez[:rows])
                    total = sum(forward_buf[turn, a, x].astype(jnp.float32) * own_e[a] for a in range(3))
                    if turn > 0:
                        total = total + masked[x]
                    if last:
                        total = total * mask[x].astype(jnp.float32)
                        for a in range(3):
                            final[a, x] = own_e[a]
                    masked[x] = total
            held_y, held_z = hy, hz


def band(rounds, total, offsets, taps, *refs):
    *blocks, out, line = refs
    width = out.shape[0]
    at_x = lax.axis_index("gx")
    core = lax.rem(at_x, 2)
    for p in range(2 * rounds + 1):
        for x in range(width):
            line[(2 * p + core) * width + x] = blocks[2 * p][x]
            line[(2 * p + 1 - core) * width + x] = blocks[2 * p + 1][x]
    origin = (2 * rounds + core) * width
    for x in range(width):
        result = None
        for b in range(offsets.shape[0]):
            place = at_x * width + x + offsets[b]
            inside = (place >= 0) & (place < total)
            weight = jnp.where(inside, taps[b], 0.0)
            term = weight * line[origin + x + offsets[b]]
            result = term if result is None else result + term
        out[x] = result


def shards(routes, adjoint_fields, forward_e, permittivity, design_mask, band_offsets, filter_taps):
    width, rows, lanes = permittivity.shape
    margin = ITERS
    f32 = jnp.float32
    planes = sum(depths(margin))
    shape = jax.ShapeDtypeStruct
    vmem = pl.BlockSpec(memory_space=pltpu.VMEM)
    smem = pl.BlockSpec(memory_space=pltpu.SMEM)
    anywhere = pl.BlockSpec(memory_space=pl.ANY)
    params = pltpu.CompilerParams(vmem_limit_bytes=24 * 1024 * 1024)
    strip = shape((planes, rows, lanes), f32)
    edge = shape((7, width // 2, SUB, lanes), f32)
    corner = shape((7, margin // 2, SUB, lanes), f32)
    out_x, in_x, side_a, side_b, diag_a, diag_b = pl.pallas_call(
        functools.partial(pack, margin),
        out_shape=(strip, strip, edge, edge, corner, corner),
        in_specs=[vmem] * 2,
        out_specs=(vmem,) * 6,
        compiler_params=params,
        name="pack_borders",
    )(adjoint_fields, permittivity)

    def move(value, pairs):
        return lax.ppermute(value, BOTH, pairs)

    out_x = move(out_x, routes.out_x)
    side_a = move(side_a, routes.side_a)
    side_b = move(side_b, routes.side_b)
    diag_a = move(diag_a, routes.diag_a)
    diag_b = move(diag_b, routes.diag_b)
    in_x = move(in_x, routes.core)
    core_a = move(side_a, routes.core)
    core_b = move(side_b, routes.core)
    masked, final = pl.pallas_call(
        functools.partial(steps, margin, routes.count_x, routes.count_y),
        out_shape=(shape((width, rows, lanes), f32), shape((3, width, rows, lanes), f32)),
        in_specs=[anywhere, vmem, anywhere, vmem] + [vmem] * 8,
        out_specs=(vmem, vmem),
        scratch_shapes=[
            pltpu.VMEM((6, width + 2 * margin, rows + SUB, lanes), f32),
            pltpu.VMEM((width + 2 * margin, rows + SUB, lanes), f32),
            pltpu.SemaphoreType.DMA,
            pltpu.VMEM(forward_e.shape, forward_e.dtype),
            pltpu.SemaphoreType.DMA,
        ],
        compiler_params=params,
        name="yee_steps",
    )(adjoint_fields, permittivity, forward_e, design_mask, out_x, in_x, side_a, side_b, diag_a, diag_b, core_a, core_b)

    total = width * routes.count_x
    rounds = -(-(total // 4) // (2 * width))
    odd_pair = lax.rem(lax.axis_index("gx") // 2, 2) == 1
    near = {0: (masked, move(masked, routes.core))}
    via_a, via_b = masked, masked
    for r in range(1, rounds + 1):
        via_a, via_b = move(via_b, routes.pair_a), move(via_a, routes.pair_b)
        core_via_a, core_via_b = move(via_a, routes.core), move(via_b, routes.core)
        near[r] = (via_a, core_via_a, via_b, core_via_b)
    blocks = []
    for p in range(-rounds, rounds + 1):
        if p == 0:
            blocks += list(near[0])
        else:
            a, core_a, b, core_b = near[abs(p)]
            flip = odd_pair if p > 0 else ~odd_pair
            blocks += [jnp.where(flip, b, a), jnp.where(flip, core_b, core_a)]
    filtered = pl.pallas_call(
        functools.partial(band, rounds, total),
        out_shape=shape((width, rows, lanes), f32),
        in_specs=[smem, smem] + [vmem] * len(blocks),
        out_specs=vmem,
        scratch_shapes=[pltpu.VMEM((len(blocks) * width, rows, lanes), f32)],
        compiler_params=params,
        name="band_filter",
    )(band_offsets, filter_taps, *blocks)
    return filtered, final


def solution(mesh):
    routes = Routes(mesh.shape["gx"], mesh.shape["gy"])
    return jax.shard_map(
        functools.partial(shards, routes),
        mesh=mesh,
        in_specs=(
            P(None, "gx", "gy", None),
            P(None, None, "gx", "gy", None),
            P("gx", "gy", None),
            P("gx", "gy", None),
            P(),
            P(),
        ),
        out_specs=(P("gx", "gy", None), P(None, "gx", "gy", None)),
        check_vma=False,
    )
```

```python
import functools
import jax
import jax.numpy as jnp
from jax import lax
from jax.experimental import pallas as pl
from jax.experimental.pallas import tpu as pltpu
from jax.sharding import PartitionSpec as P

ITERS = 4
COURANT = 0.5
BOTH = ("gx", "gy")
SUB = 8


def swaps(count_x, count_y, partner, idle):
    pairs = []
    for x in range(count_x):
        for y in range(count_y):
            to = partner(x, y)
            if to is None:
                to = idle(x, y)
            pairs.append((x * count_y + y, to[0] * count_y + to[1]))
    assert sorted(b for _, b in pairs) == sorted(a for a, _ in pairs)
    return pairs


class Routes:
    def __init__(self, count_x, count_y):
        self.count_x, self.count_y = count_x, count_y
        half = max(count_y // 2, 1)

        def outward_x(x):
            to = x + 1 if x % 2 else x - 1
            return to if 0 <= to < count_x else None

        def side_b(y):
            to = y + 1 if y % 2 else y - 1
            return to if 0 <= to < count_y else None

        def far_y(x, y):
            return (x, (y + half) % count_y)

        def out_partner(x, y):
            return None if outward_x(x) is None else (outward_x(x), y)

        def b_partner(x, y):
            return None if side_b(y) is None else (x, side_b(y))

        def pair_b(x, y):
            to = (x // 2 + (1 if (x // 2) % 2 else -1)) * 2 + x % 2
            return (to, y) if 0 <= to < count_x else None

        make = functools.partial(swaps, count_x, count_y)
        core = lambda x, y: (x ^ 1, y)
        self.core = make(core, None)
        self.out_x = make(out_partner, far_y)
        self.side_a = make(lambda x, y: (x, y ^ 1), None)
        self.side_b = make(b_partner, core)
        self.pair_a = make(lambda x, y: (x ^ 2, y), None)
        self.pair_b = make(pair_b, core)


def depths(margin):
    return (margin, margin, margin, margin - 1, margin, margin, margin - 1)


def edge_tile(low, first, second, upper):
    up = upper == 1
    first = jnp.where(up, pltpu.roll(first, SUB // 2, 0), first)
    second = jnp.where(up, second, pltpu.roll(second, SUB // 2, 0))
    return jnp.where(low, first, second)


def tail_tile(low, odd, from_a, from_b, upper):
    after = jnp.where(odd == 0, from_a, from_b)
    before = jnp.where(odd == 0, from_b, from_a)
    if upper:
        after = pltpu.roll(after, SUB // 2, 0)
    else:
        before = pltpu.roll(before, SUB // 2, 0)
    return jnp.where(low, after, before)


def low_half(lanes):
    return lax.broadcasted_iota(jnp.int32, (SUB, lanes), 0) < SUB // 2


def position():
    at_x, at_y = lax.axis_index("gx"), lax.axis_index("gy")
    return at_x, at_y, lax.rem(at_x, 2), lax.rem(at_y, 2)


def pack(margin, fields, perm, ext, out_x, in_x, side_a, side_b, sems):
    width, rows, lanes = perm.shape
    _, _, core, odd = position()
    low = low_half(lanes)
    own = (pl.ds(margin, width), pl.ds(0, rows))
    loads = [pltpu.make_async_copy(fields.at[k], ext.at[(k, *own)], sems.at[k]) for k in range(6)]
    loads.append(pltpu.make_async_copy(perm, ext.at[(6, *own)], sems.at[6]))
    for load in loads:
        load.start()
    at = 0
    for k, depth in enumerate(depths(margin)):
        loads[k].wait()
        for j in range(depth):
            out_x[at + j] = ext[k, margin + core * (width - depth) + j, 0:rows]
            in_x[at + j] = ext[k, margin + (1 - core) * (width - depth) + j, 0:rows]
        at += depth

        def edge(x, x2, upper):
            where = pl.ds(pl.multiple_of(upper * (rows - SUB), SUB), SUB)
            return edge_tile(low, ext[k, margin + x, where], ext[k, margin + x2, where], upper)

        for j in range(width // 2):
            side_a[k, j] = edge(j, j + width // 2, 1 - odd)
            side_b[k, j] = edge(j, j + width // 2, odd)


def tails(margin, count_y, ext_in, side_a, side_b, ext, inner, outer):
    del ext_in
    width, rows, lanes = ext.shape[1] - 2 * margin, ext.shape[2] - SUB, ext.shape[3]
    _, at_y, core, odd = position()
    low = low_half(lanes)
    valid = jnp.where(low, jnp.where(at_y < count_y - 1, 1, 0), jnp.where(at_y > 0, 1, 0)) > 0
    for k in range(7):
        for x in range(width):
            j, upper = x % (width // 2), x // (width // 2)
            tile = tail_tile(low, odd, side_a[k, j], side_b[k, j], upper)
            ext[k, margin + x, rows:] = jnp.where(valid, tile, 1.0 if k == 6 else 0.0)
        for j in range(margin):
            inner[k, j] = ext[k, margin + (1 - core) * (width - margin) + j, rows:]
            outer[k, j] = ext[k, margin + core * (width - margin) + j, rows:]


def steps(margin, reach, count_x, count_y, ext_in, forward, mask, out_x, in_x, inner, outer, offsets, taps,
          ext, masked, final, weights, table, table_sems):
    del ext_in
    width, rows, lanes = mask.shape
    high = rows + SUB
    at_x, at_y, core, odd = position()
    load_offsets = pltpu.make_async_copy(offsets, table[0], table_sems.at[0])
    load_taps = pltpu.make_async_copy(taps, table[1], table_sems.at[1])
    load_offsets.start()
    load_taps.start()

    scale = COURANT * COURANT
    low = low_half(lanes)
    has_out = jnp.where(core == 0, at_x > 0, at_x < count_x - 1)
    has_after, has_before = at_y < count_y - 1, at_y > 0
    valid_y = jnp.where(low, jnp.where(has_after, 1, 0), jnp.where(has_before, 1, 0)) > 0
    valid_corner = valid_y & jnp.broadcast_to(has_out, (SUB, lanes))
    out_at = core * (width + margin)
    in_at = (1 - core) * (width + margin)

    def put(k, x, where, value, valid):
        if k == 6:
            value = scale / value
        ext[k, x, where] = value if valid is None else jnp.where(valid, value, 0.0)

    body, tail = pl.ds(0, rows), pl.ds(rows, SUB)
    for x in range(margin, margin + width):
        put(6, x, body, ext[6, x, 0:rows], None)
        put(6, x, tail, ext[6, x, rows:], valid_y)
    at = 0
    for k, depth in enumerate(depths(margin)):
        for j in range(depth):
            put(k, out_at + (1 - core) * (margin - depth) + j, body, out_x[at + j], has_out)
            put(k, in_at + core * (margin - depth) + j, body, in_x[at + j], None)
        at += depth
    for k in range(7):
        for j in range(margin):
            put(k, out_at + j, tail, outer[k, j], valid_corner if k == 6 else has_out)
            put(k, in_at + j, tail, inner[k, j], valid_y if k == 6 else None)

    lane = lax.broadcasted_iota(jnp.int32, (high, lanes), 1)
    first_lane = lane == 0
    before_rows = jnp.where(low | jnp.broadcast_to(has_before, (SUB, lanes)), 1.0, 0.0)
    before_x = jnp.where(at_x > 0, 1.0, 0.0)

    gap = lax.broadcasted_iota(jnp.int32, (lanes, lanes), 0) - lax.broadcasted_iota(jnp.int32, (lanes, lanes), 1)
    ahead = jnp.where(gap == 1, 1.0, 0.0) - jnp.where(gap == 0, 1.0, 0.0)
    ahead = jnp.concatenate([ahead, ahead], 0).astype(jnp.bfloat16)

    def ahead_z(k, first, end):
        f = ext[k, first:end].reshape((end - first) * high, lanes)
        main = f.astype(jnp.bfloat16)
        rest = (f - main.astype(jnp.float32)).astype(jnp.bfloat16)
        return jnp.dot(jnp.concatenate([main, rest], 1), ahead, preferred_element_type=jnp.float32)

    def next_y(f):
        return pltpu.roll(f, high - 1, 0)

    def last_y(f):
        return pltpu.roll(f, 1, 0)

    def last_z(f):
        return jnp.where(first_lane, 0.0, pltpu.roll(f, 1, 1))

    for turn in range(margin):
        last = turn == margin - 1
        first, end = turn, width + 2 * margin - 1 - turn
        ahead_x, ahead_y = ahead_z(0, first, end), ahead_z(1, first, end)
        held_y = held_z = None
        for i in range(first, end):
            ex, ey, ez = ext[0, i], ext[1, i], ext[2, i]
            ey_x, ez_x = ext[1, i + 1], ext[2, i + 1]
            hx, hy, hz = ext[3, i], ext[4, i], ext[5, i]
            if turn == 0:
                hx, hy, hz = hx * (1 / COURANT), hy * (1 / COURANT), hz * (1 / COURANT)
            here = slice((i - first) * high, (i - first + 1) * high)
            hx = hx - ((next_y(ez) - ez) - ahead_y[here])
            hy = hy - (ahead_x[here] - (ez_x - ez))
            hz = hz - ((ey_x - ey) - (next_y(ex) - ex))

            def clear(h):
                h = jnp.concatenate([h[:rows], h[rows:] * before_rows], 0)
                return h * before_x if i < margin else h

            hx, hy, hz = clear(hx), clear(hy), clear(hz)
            if not last:
                ext[3, i], ext[4, i], ext[5, i] = hx, hy, hz
            if i > first:
                c = ext[6, i]
                ex = ex + c * ((hz - last_y(hz)) - (hy - last_z(hy)))
                ey = ey + c * ((hx - last_z(hx)) - (hz - held_z))
                ez = ez + c * ((hy - held_y) - (hx - last_y(hx)))
                if not last:
                    ext[0, i], ext[1, i], ext[2, i] = ex, ey, ez
                if margin <= i < margin + width:
                    x = i - margin
                    own_e = (ex[:rows], ey[:rows], ez[:rows])
                    total = sum(forward[turn, a, x].astype(jnp.float32) * own_e[a] for a in range(3))
                    if turn > 0:
                        total = total + masked[x]
                    if last:
                        total = total * mask[x].astype(jnp.float32)
                        for a in range(3):
                            final[a, x] = own_e[a]
                    masked[x] = total
            held_y, held_z = hy, hz

    load_offsets.wait()
    load_taps.wait()
    distance = lax.broadcasted_iota(jnp.int32, weights.shape, 0) - reach
    total = jnp.zeros(weights.shape, jnp.float32)
    for b in range(offsets.shape[0]):
        total = total + jnp.where(distance == table[0][b], table[1][b], 0.0)
    weights[...] = total


def band(rounds, reach, count_x, weights, own, other, *refs):
    *near, out = refs
    width, rows, lanes = out.shape
    at_x, _, core, _ = position()
    pair = at_x // 2
    even = lax.rem(pair, 2) == 0

    def value(k, x, where):
        def of_pair(p, same):
            if p == 0:
                return (own if same else other)[x, where]
            a, b, core_a, core_b = near[4 * (abs(p) - 1) : 4 * abs(p)]
            first, second = (a, b) if same else (core_a, core_b)
            found = jnp.where(even == (p > 0), first[x, where], second[x, where])
            return jnp.where((pair + p >= 0) & (pair + p < count_x // 2), found, 0.0)

        if k % 2 == 0:
            return of_pair(k // 2, True)
        return jnp.where(core == 0, of_pair((k - 1) // 2, False), of_pair((k + 1) // 2, False))

    for r in range(rows // SUB):
        where = slice(r * SUB, (r + 1) * SUB)
        line = {}
        sums = [None] * width
        for d in range(-reach, reach + 1):
            weight = jnp.broadcast_to(weights[d + reach : d + reach + 1], (SUB, lanes))
            for x in range(width):
                at = x + d
                if at not in line:
                    line[at] = value(at // width, at % width, where)
                term = weight * line[at]
                sums[x] = term if sums[x] is None else sums[x] + term
        for x in range(width):
            out[x, where] = sums[x]


def shards(routes, adjoint_fields, forward_e, permittivity, design_mask, band_offsets, filter_taps):
    width, rows, lanes = permittivity.shape
    margin = ITERS
    f32 = jnp.float32
    planes = sum(depths(margin))
    shape = jax.ShapeDtypeStruct
    vmem = pl.BlockSpec(memory_space=pltpu.VMEM)
    hbm = pl.BlockSpec(memory_space=pltpu.HBM)
    params = pltpu.CompilerParams(vmem_limit_bytes=24 * 1024 * 1024)
    block = shape((width, rows, lanes), f32)
    ext = shape((7, width + 2 * margin, rows + SUB, lanes), f32)
    strip = shape((planes, rows, lanes), f32)
    edge = shape((7, width // 2, SUB, lanes), f32)
    inner = shape((7, margin, SUB, lanes), f32)
    cells, out_x, in_x, side_a, side_b = pl.pallas_call(
        functools.partial(pack, margin),
        out_shape=(ext, strip, strip, edge, edge),
        in_specs=[hbm] * 2,
        out_specs=(vmem,) * 5,
        scratch_shapes=[pltpu.SemaphoreType.DMA((7,))],
        compiler_params=params,
        name="pack_borders",
    )(pltpu.with_memory_space_constraint(adjoint_fields, pltpu.HBM), pltpu.with_memory_space_constraint(permittivity, pltpu.HBM))

    def move(value, pairs):
        return lax.ppermute(value, BOTH, pairs)

    in_x = move(in_x, routes.core)
    side_b = move(side_b, routes.side_b)
    out_x = move(out_x, routes.out_x)
    side_a = move(side_a, routes.side_a)
    cells, inner, outer = pl.pallas_call(
        functools.partial(tails, margin, routes.count_y),
        out_shape=(ext, inner, inner),
        in_specs=[vmem] * 3,
        out_specs=(vmem,) * 3,
        input_output_aliases={0: 0},
        compiler_params=params,
        name="join_sides",
    )(cells, side_a, side_b)
    outer = move(outer, routes.out_x)
    inner = move(inner, routes.core)
    reach = width * routes.count_x // 4
    rounds = -(-reach // (2 * width))
    _, masked, final, weights = pl.pallas_call(
        functools.partial(steps, margin, reach, routes.count_x, routes.count_y),
        out_shape=(ext, block, shape((3, width, rows, lanes), f32), shape((-(-(2 * reach + 1) // SUB) * SUB, lanes), f32)),
        in_specs=[vmem] * 7 + [hbm] * 2,
        out_specs=(vmem,) * 4,
        input_output_aliases={0: 0},
        scratch_shapes=[
            (pltpu.SMEM(band_offsets.shape, band_offsets.dtype), pltpu.SMEM(filter_taps.shape, filter_taps.dtype)),
            pltpu.SemaphoreType.DMA((2,)),
        ],
        compiler_params=params,
        name="yee_steps",
    )(cells, forward_e, design_mask, out_x, in_x, inner, outer, band_offsets, filter_taps)

    other = move(masked, routes.core)
    via_a, via_b = masked, masked
    near = []
    for _ in range(rounds):
        via_a, via_b = move(via_b, routes.pair_a), move(via_a, routes.pair_b)
        near += [via_a, via_b, move(via_a, routes.core), move(via_b, routes.core)]
    filtered = pl.pallas_call(
        functools.partial(band, rounds, reach, routes.count_x),
        out_shape=block,
        in_specs=[vmem] * (3 + len(near)),
        out_specs=vmem,
        compiler_params=params,
        name="band_filter",
    )(weights, masked, other, *near)
    return filtered, final


def solution(mesh):
    routes = Routes(mesh.shape["gx"], mesh.shape["gy"])
    return jax.shard_map(
        functools.partial(shards, routes),
        mesh=mesh,
        in_specs=(
            P(None, "gx", "gy", None),
            P(None, None, "gx", "gy", None),
            P("gx", "gy", None),
            P("gx", "gy", None),
            P(),
            P(),
        ),
        out_specs=(P("gx", "gy", None), P(None, "gx", "gy", None)),
        check_vma=False,
    )
```

```python
import functools
import jax
import jax.numpy as jnp
from jax import lax
from jax.experimental import pallas as pl
from jax.experimental.pallas import tpu as pltpu
from jax.sharding import PartitionSpec as P

ITERS = 4
COURANT = 0.5
BOTH = ("gx", "gy")
SUB = 8
JOIN_Y_US = 50
JOIN_X_US = 0.05
BAND_OWN_US = 2


def swaps(count_x, count_y, partner, idle):
    pairs = []
    for x in range(count_x):
        for y in range(count_y):
            to = partner(x, y)
            if to is None:
                to = idle(x, y)
            pairs.append((x * count_y + y, to[0] * count_y + to[1]))
    assert sorted(b for _, b in pairs) == sorted(a for a, _ in pairs)
    return pairs


class Routes:
    def __init__(self, count_x, count_y):
        self.count_x, self.count_y = count_x, count_y
        half = max(count_y // 2, 1)

        def outward_x(x):
            to = x + 1 if x % 2 else x - 1
            return to if 0 <= to < count_x else None

        def side_b(y):
            to = y + 1 if y % 2 else y - 1
            return to if 0 <= to < count_y else None

        def far_y(x, y):
            return (x, (y + half) % count_y)

        def out_partner(x, y):
            return None if outward_x(x) is None else (outward_x(x), y)

        def b_partner(x, y):
            return None if side_b(y) is None else (x, side_b(y))

        def ring(x, y, up):
            to = x + 2 if x % 2 == up else x - 2
            return (to, y) if 0 <= to < count_x else (x ^ 1, y)

        make = functools.partial(swaps, count_x, count_y)
        core = lambda x, y: (x ^ 1, y)
        self.core = make(core, None)
        self.out_x = make(out_partner, far_y)
        self.side_a = make(lambda x, y: (x, y ^ 1), None)
        self.side_b = make(b_partner, core)
        self.ring_1 = make(lambda x, y: ring(x, y, 1), None)
        self.ring_0 = make(lambda x, y: ring(x, y, 0), None)


def depths(margin):
    return (margin, margin, margin, margin - 1, margin, margin, margin - 1)


def edge_tile(low, first, second, upper):
    up = upper == 1
    first = jnp.where(up, pltpu.roll(first, SUB // 2, 0), first)
    second = jnp.where(up, second, pltpu.roll(second, SUB // 2, 0))
    return jnp.where(low, first, second)


def tail_tile(low, odd, from_a, from_b, upper):
    after = jnp.where(odd == 0, from_a, from_b)
    before = jnp.where(odd == 0, from_b, from_a)
    if upper:
        after = pltpu.roll(after, SUB // 2, 0)
    else:
        before = pltpu.roll(before, SUB // 2, 0)
    return jnp.where(low, after, before)


def low_half(lanes):
    return lax.broadcasted_iota(jnp.int32, (SUB, lanes), 0) < SUB // 2


def position():
    at_x, at_y = lax.axis_index("gx"), lax.axis_index("gy")
    return at_x, at_y, lax.rem(at_x, 2), lax.rem(at_y, 2)


def pack_y(margin, fields, perm, ext, side_a, side_b, sems):
    width, rows, lanes = perm.shape
    _, _, _, odd = position()
    low = low_half(lanes)
    own = (pl.ds(margin, width), pl.ds(0, rows))
    loads = [pltpu.make_async_copy(fields.at[k] if k < 6 else perm, ext.at[(k, *own)], sems.at[k]) for k in range(7)]
    for load in loads:
        load.start()
    for k in range(7):
        loads[k].wait()

        def edge(x, upper):
            where = pl.ds(pl.multiple_of(upper * (rows - SUB), SUB), SUB)
            return edge_tile(low, ext[k, margin + x, where], ext[k, margin + x + width // 2, where], upper)

        for j in range(width // 2):
            side_a[k, j] = edge(j, 1 - odd)
            side_b[k, j] = edge(j, odd)


def pack_x(margin, ext, out_x, in_x):
    width, rows = ext.shape[1] - 2 * margin, ext.shape[2] - SUB
    _, _, core, _ = position()
    at = 0
    for k, depth in enumerate(depths(margin)):
        for j in range(depth):
            out_x[at + j] = ext[k, margin + core * (width - depth) + j, 0:rows]
            in_x[at + j] = ext[k, margin + (1 - core) * (width - depth) + j, 0:rows]
        at += depth


def valid_rows(low, at_y, count_y):
    return jnp.where(low, jnp.where(at_y < count_y - 1, 1, 0), jnp.where(at_y > 0, 1, 0)) > 0


def has_outward(at_x, core, count_x):
    return jnp.where(core == 0, at_x > 0, at_x < count_x - 1)


def join_y(margin, count_y, ext_in, side_a, side_b, ext, outer):
    del ext_in
    width, rows, lanes = ext.shape[1] - 2 * margin, ext.shape[2] - SUB, ext.shape[3]
    _, at_y, core, odd = position()
    low = low_half(lanes)
    valid = valid_rows(low, at_y, count_y)
    for k in range(7):
        for x in range(width):
            j, upper = x % (width // 2), x // (width // 2)
            tile = tail_tile(low, odd, side_a[k, j], side_b[k, j], upper)
            ext[k, margin + x, rows:] = jnp.where(valid, tile, 1.0 if k == 6 else 0.0)
        for j in range(margin):
            outer[k, j] = ext[k, margin + core * (width - margin) + j, rows:]


def join_inner(margin, count_y, ext_in, ext, inner):
    del ext_in
    width, rows, lanes = ext.shape[1] - 2 * margin, ext.shape[2] - SUB, ext.shape[3]
    _, at_y, core, _ = position()
    valid = valid_rows(low_half(lanes), at_y, count_y)
    for k in range(7):
        for j in range(margin):
            inner[k, j] = ext[k, margin + (1 - core) * (width - margin) + j, rows:]
    scale = COURANT * COURANT
    for x in range(margin, margin + width):
        ext[6, x, 0:rows] = scale / ext[6, x, 0:rows]
        ext[6, x, rows:] = jnp.where(valid, scale / ext[6, x, rows:], 0.0)


def load_rest(ext_in, forward, mask, offsets, taps, ext, forward_out, mask_out, weights, table, sems):
    del ext_in, ext
    lists = [pltpu.make_async_copy(offsets, table[0], sems.at[0]), pltpu.make_async_copy(taps, table[1], sems.at[1])]
    loads = [pltpu.make_async_copy(forward, forward_out, sems.at[2]), pltpu.make_async_copy(mask, mask_out, sems.at[3])]
    for load in lists + loads:
        load.start()
    for load in lists:
        load.wait()
    distance = lax.broadcasted_iota(jnp.int32, weights.shape, 0) - weights.shape[0] // 2
    total = jnp.zeros(weights.shape, jnp.float32)
    for b in range(offsets.shape[0]):
        total = total + jnp.where(distance == table[0][b], table[1][b], 0.0)
    weights[...] = total
    for load in loads:
        load.wait()


def join_core(margin, ext_in, in_x, ext):
    del ext_in
    width, rows = ext.shape[1] - 2 * margin, ext.shape[2] - SUB
    _, _, core, _ = position()
    in_at = (1 - core) * (width + margin)
    at = 0
    for k, depth in enumerate(depths(margin)):
        for j in range(depth):
            plane = in_x[at + j]
            plane = COURANT * COURANT / plane if k == 6 else plane
            ext[k, in_at + core * (margin - depth) + j, 0:rows] = plane
        at += depth


def join_outer(margin, count_x, ext_in, out_x, ext):
    del ext_in
    width, rows = ext.shape[1] - 2 * margin, ext.shape[2] - SUB
    at_x, _, core, _ = position()
    has_out = has_outward(at_x, core, count_x)
    out_at = core * (width + margin)
    at = 0
    for k, depth in enumerate(depths(margin)):
        for j in range(depth):
            plane = out_x[at + j]
            plane = COURANT * COURANT / plane if k == 6 else plane
            ext[k, out_at + (1 - core) * (margin - depth) + j, 0:rows] = jnp.where(has_out, plane, 0.0)
        at += depth


def join_corner(margin, count_x, count_y, ext_in, outer, ext):
    del ext_in
    width, rows, lanes = ext.shape[1] - 2 * margin, ext.shape[2] - SUB, ext.shape[3]
    at_x, at_y, core, _ = position()
    has_out = has_outward(at_x, core, count_x)
    valid = valid_rows(low_half(lanes), at_y, count_y) & jnp.broadcast_to(has_out, (SUB, lanes))
    out_at = core * (width + margin)
    for k in range(7):
        for j in range(margin):
            tile = outer[k, j]
            tile = jnp.where(valid, COURANT * COURANT / tile, 0.0) if k == 6 else jnp.where(has_out, tile, 0.0)
            ext[k, out_at + j, rows:] = tile


def steps(margin, count_x, count_y, ext_in, forward, mask, inner, ext, masked, final):
    del ext_in
    width, rows, lanes = mask.shape
    high = rows + SUB
    at_x, at_y, core, _ = position()
    low = low_half(lanes)
    has_before = at_y > 0
    valid = valid_rows(low, at_y, count_y)
    in_at = (1 - core) * (width + margin)
    for k in range(7):
        for j in range(margin):
            tile = inner[k, j]
            ext[k, in_at + j, rows:] = jnp.where(valid, COURANT * COURANT / tile, 0.0) if k == 6 else tile

    lane = lax.broadcasted_iota(jnp.int32, (high, lanes), 1)
    first_lane = lane == 0
    before_rows = jnp.where(low | jnp.broadcast_to(has_before, (SUB, lanes)), 1.0, 0.0)
    before_x = jnp.where(at_x > 0, 1.0, 0.0)

    gap = lax.broadcasted_iota(jnp.int32, (lanes, lanes), 0) - lax.broadcasted_iota(jnp.int32, (lanes, lanes), 1)
    ahead = jnp.where(gap == 1, 1.0, 0.0) - jnp.where(gap == 0, 1.0, 0.0)
    ahead = jnp.concatenate([ahead, ahead], 0).astype(jnp.bfloat16)

    def ahead_z(k, first, end):
        f = ext[k, first:end].reshape((end - first) * high, lanes)
        main = f.astype(jnp.bfloat16)
        rest = (f - main.astype(jnp.float32)).astype(jnp.bfloat16)
        return jnp.dot(jnp.concatenate([main, rest], 1), ahead, preferred_element_type=jnp.float32)

    def next_y(f):
        return pltpu.roll(f, high - 1, 0)

    def last_y(f):
        return pltpu.roll(f, 1, 0)

    def last_z(f):
        return jnp.where(first_lane, 0.0, pltpu.roll(f, 1, 1))

    for turn in range(margin):
        last = turn == margin - 1
        first, end = turn, width + 2 * margin - 1 - turn
        ahead_x, ahead_y = ahead_z(0, first, end), ahead_z(1, first, end)
        held_y = held_z = None
        for i in range(first, end):
            ex, ey, ez = ext[0, i], ext[1, i], ext[2, i]
            ey_x, ez_x = ext[1, i + 1], ext[2, i + 1]
            hx, hy, hz = ext[3, i], ext[4, i], ext[5, i]
            if turn == 0:
                hx, hy, hz = hx * (1 / COURANT), hy * (1 / COURANT), hz * (1 / COURANT)
            here = slice((i - first) * high, (i - first + 1) * high)
            hx = hx - ((next_y(ez) - ez) - ahead_y[here])
            hy = hy - (ahead_x[here] - (ez_x - ez))
            hz = hz - ((ey_x - ey) - (next_y(ex) - ex))

            def clear(h):
                h = jnp.concatenate([h[:rows], h[rows:] * before_rows], 0)
                return h * before_x if i < margin else h

            hx, hy, hz = clear(hx), clear(hy), clear(hz)
            if not last:
                ext[3, i], ext[4, i], ext[5, i] = hx, hy, hz
            if i > first:
                c = ext[6, i]
                ex = ex + c * ((hz - last_y(hz)) - (hy - last_z(hy)))
                ey = ey + c * ((hx - last_z(hx)) - (hz - held_z))
                ez = ez + c * ((hy - held_y) - (hx - last_y(hx)))
                if not last:
                    ext[0, i], ext[1, i], ext[2, i] = ex, ey, ez
                if margin <= i < margin + width:
                    x = i - margin
                    own_e = (ex[:rows], ey[:rows], ez[:rows])
                    total = sum(forward[turn, a, x].astype(jnp.float32) * own_e[a] for a in range(3))
                    if turn > 0:
                        total = total + masked[x]
                    if last:
                        total = total * mask[x].astype(jnp.float32)
                        for a in range(3):
                            final[a, x] = own_e[a]
                    masked[x] = total
            held_y, held_z = hy, hz


def band_sum(reach, hop, sign, alone, weights, own, other, where, sums):
    width, _, lanes = own.shape
    _, _, core, _ = position()
    middle = weights.shape[0] // 2
    for j in range(width):
        for same in (True,) if alone else (True, False):
            plane = (own if same else other)[j, where]
            for x in range(width):
                distances = [j - x - 2 * hop * s * width + (0 if same else t * width) for s in (1, -1) for t in (1, -1)]
                if min(abs(distance) for distance in distances) > reach:
                    continue
                distance = j - x - 2 * hop * width * sign + (0 if same else (1 - 2 * core) * width)
                weight = jnp.broadcast_to(weights[pl.ds(middle + distance, 1)], (SUB, lanes))
                sums[x] = sums[x] + weight * plane
    return sums


def arrived(count_x, via_1, via_0, x, where):
    at_x, _, core, _ = position()
    first, second = via_1[x, where], via_0[x, where]
    up = core == 1
    before = jnp.where(at_x >= 2, jnp.where(up, first, second), 0.0)
    after = jnp.where(at_x < count_x - 2, jnp.where(up, second, first), 0.0)
    return before, after


def band_hop(reach, hop, count_x, up, alone, weights, own, *refs):
    *refs, send = refs
    other, via = (own, refs) if alone else (refs[0], refs[1:])
    width, rows, lanes = own.shape
    _, _, core, _ = position()
    ahead = core == up
    for r in range(rows // SUB):
        where = slice(r * SUB, (r + 1) * SUB)
        if via:
            start = [jnp.where(ahead, *arrived(count_x, *via, x, where)) for x in range(width)]
        else:
            start = [jnp.zeros((SUB, lanes), jnp.float32)] * width
        sums = band_sum(reach, hop, jnp.where(ahead, 1, -1), alone, weights, own, other, where, start)
        for x in range(width):
            send[x, where] = sums[x]


def band_own(reach, weights, own, other, final, base, stored, sem):
    store = pltpu.make_async_copy(final, stored, sem)
    store.start()
    width, rows, lanes = own.shape
    for r in range(rows // SUB):
        where = slice(r * SUB, (r + 1) * SUB)
        sums = band_sum(reach, 0, 1, False, weights, own, other, where, [jnp.zeros((SUB, lanes), jnp.float32)] * width)
        for x in range(width):
            base[x, where] = sums[x]
    store.wait()


def band_end(count_x, base, via_1, via_0, out):
    for x in range(out.shape[0]):
        before, after = arrived(count_x, via_1, via_0, x, slice(None))
        out[x] = base[x] + before + after


def shards(routes, adjoint_fields, forward_e, permittivity, design_mask, band_offsets, filter_taps):
    width, rows, lanes = permittivity.shape
    margin = ITERS
    f32 = jnp.float32
    planes = sum(depths(margin))
    shape = jax.ShapeDtypeStruct
    vmem = pl.BlockSpec(memory_space=pltpu.VMEM)
    hbm = pl.BlockSpec(memory_space=pltpu.HBM)
    params = pltpu.CompilerParams(vmem_limit_bytes=24 * 1024 * 1024)
    block = shape((width, rows, lanes), f32)
    ext = shape((7, width + 2 * margin, rows + SUB, lanes), f32)
    strip = shape((planes, rows, lanes), f32)
    edge = shape((7, width // 2, SUB, lanes), f32)
    corner = shape((7, margin, SUB, lanes), f32)
    reach = width * routes.count_x // 4
    rounds = -(-reach // (2 * width))
    distances = shape((4 * (rounds + 1) * width, lanes), f32)

    def cost(microseconds):
        return pl.CostEstimate(flops=int(microseconds * 1e9), bytes_accessed=int(microseconds * 3.6e6), transcendentals=0)

    def move(value, pairs):
        return lax.ppermute(value, BOTH, pairs)

    def from_hbm(*values):
        return [pltpu.with_memory_space_constraint(value, pltpu.HBM) for value in values]

    cells, side_a, side_b = pl.pallas_call(
        functools.partial(pack_y, margin),
        out_shape=(ext, edge, edge),
        in_specs=[hbm] * 2,
        out_specs=(vmem,) * 3,
        scratch_shapes=[pltpu.SemaphoreType.DMA((7,))],
        compiler_params=params,
        name="pack_y",
    )(*from_hbm(adjoint_fields, permittivity))
    out_x, in_x = pl.pallas_call(
        functools.partial(pack_x, margin),
        out_shape=(strip, strip),
        in_specs=[vmem],
        out_specs=(vmem,) * 2,
        compiler_params=params,
        name="pack_x",
    )(cells)
    side_b = move(side_b, routes.side_b)
    side_a = move(side_a, routes.side_a)
    in_x = move(in_x, routes.core)
    out_x = move(out_x, routes.out_x)
    cells, forward_e, design_mask, weights = pl.pallas_call(
        load_rest,
        out_shape=(ext, pltpu.VMEM(forward_e.shape, forward_e.dtype), pltpu.VMEM(design_mask.shape, design_mask.dtype), distances),
        in_specs=[vmem] + [hbm] * 4,
        out_specs=(vmem,) * 4,
        input_output_aliases={0: 0},
        scratch_shapes=[
            (pltpu.SMEM(band_offsets.shape, band_offsets.dtype), pltpu.SMEM(filter_taps.shape, filter_taps.dtype)),
            pltpu.SemaphoreType.DMA((4,)),
        ],
        compiler_params=params,
        cost_estimate=cost(JOIN_X_US),
        name="load_rest",
    )(cells, *from_hbm(forward_e, design_mask, band_offsets, filter_taps))
    cells, outer = pl.pallas_call(
        functools.partial(join_y, margin, routes.count_y),
        out_shape=(ext, corner),
        in_specs=[vmem] * 3,
        out_specs=(vmem,) * 2,
        input_output_aliases={0: 0},
        compiler_params=params,
        cost_estimate=cost(JOIN_Y_US),
        name="join_y",
    )(cells, side_a, side_b)
    outer = move(outer, routes.out_x)
    cells, inner = pl.pallas_call(
        functools.partial(join_inner, margin, routes.count_y),
        out_shape=(ext, corner),
        in_specs=[vmem],
        out_specs=(vmem,) * 2,
        input_output_aliases={0: 0},
        compiler_params=params,
        cost_estimate=cost(JOIN_X_US),
        name="join_inner",
    )(cells)
    inner = move(inner, routes.core)
    cells = pl.pallas_call(
        functools.partial(join_outer, margin, routes.count_x),
        out_shape=ext,
        in_specs=[vmem] * 2,
        out_specs=vmem,
        input_output_aliases={0: 0},
        compiler_params=params,
        cost_estimate=cost(JOIN_X_US),
        name="join_outer",
    )(cells, out_x)
    cells = pl.pallas_call(
        functools.partial(join_core, margin),
        out_shape=ext,
        in_specs=[vmem] * 2,
        out_specs=vmem,
        input_output_aliases={0: 0},
        compiler_params=params,
        cost_estimate=cost(JOIN_X_US),
        name="join_core",
    )(cells, in_x)
    cells = pl.pallas_call(
        functools.partial(join_corner, margin, routes.count_x, routes.count_y),
        out_shape=ext,
        in_specs=[vmem] * 2,
        out_specs=vmem,
        input_output_aliases={0: 0},
        compiler_params=params,
        cost_estimate=cost(JOIN_X_US),
        name="join_corner",
    )(cells, outer)
    _, masked, final = pl.pallas_call(
        functools.partial(steps, margin, routes.count_x, routes.count_y),
        out_shape=(ext, block, pltpu.VMEM((3, width, rows, lanes), f32)),
        in_specs=[vmem] * 4,
        out_specs=(vmem,) * 3,
        input_output_aliases={0: 0},
        compiler_params=params,
        name="yee_steps",
    )(cells, forward_e, design_mask, inner)

    other = move(masked, routes.core)
    via = []

    def hop_kernel(hop, up, alone):
        operands = [weights, masked] + ([] if alone else [other]) + via
        return pl.pallas_call(
            functools.partial(band_hop, reach, hop, routes.count_x, up, alone),
            out_shape=block,
            in_specs=[vmem] * len(operands),
            out_specs=vmem,
            compiler_params=params,
            name="band_hop",
        )(*operands)

    for hop in range(rounds, 0, -1):
        send_1 = hop_kernel(hop, 1, hop == rounds)
        send_0 = hop_kernel(hop, 0, False)
        via = [move(send_1, routes.ring_1), move(send_0, routes.ring_0)]
    base, final = pl.pallas_call(
        functools.partial(band_own, reach),
        out_shape=(block, shape(final.shape, f32)),
        in_specs=[vmem] * 4,
        out_specs=(vmem, hbm),
        scratch_shapes=[pltpu.SemaphoreType.DMA],
        compiler_params=params,
        cost_estimate=cost(BAND_OWN_US),
        name="band_own",
    )(weights, masked, other, final)
    filtered = pl.pallas_call(
        functools.partial(band_end, routes.count_x),
        out_shape=block,
        in_specs=[vmem] * 3,
        out_specs=vmem,
        compiler_params=params,
        name="band_end",
    )(base, *via)
    return filtered, final


def solution(mesh):
    routes = Routes(mesh.shape["gx"], mesh.shape["gy"])
    return jax.shard_map(
        functools.partial(shards, routes),
        mesh=mesh,
        in_specs=(
            P(None, "gx", "gy", None),
            P(None, None, "gx", "gy", None),
            P("gx", "gy", None),
            P("gx", "gy", None),
            P(),
            P(),
        ),
        out_specs=(P("gx", "gy", None), P(None, "gx", "gy", None)),
        check_vma=False,
    )
```

```python
import functools
import jax
import jax.numpy as jnp
from jax import lax
from jax.experimental import pallas as pl
from jax.experimental.pallas import tpu as pltpu
from jax.sharding import PartitionSpec as P

ITERS = 4
COURANT = 0.5
BOTH = ("gx", "gy")
SUB = 8
JOIN_Y_US = 50
JOIN_X_US = 0.05
BAND_OWN_US = 2


def swaps(count_x, count_y, partner, idle):
    pairs = []
    for x in range(count_x):
        for y in range(count_y):
            to = partner(x, y)
            if to is None:
                to = idle(x, y)
            pairs.append((x * count_y + y, to[0] * count_y + to[1]))
    assert sorted(b for _, b in pairs) == sorted(a for a, _ in pairs)
    return pairs


class Routes:
    def __init__(self, count_x, count_y):
        self.count_x, self.count_y = count_x, count_y
        round_y = [y ^ (y >> 1) for y in range(count_y)]
        if sorted(round_y) != list(range(count_y)):
            round_y = list(range(count_y))

        def outward_x(x):
            to = x + 1 if x % 2 else x - 1
            return to if 0 <= to < count_x else None

        def side_b(y):
            to = y + 1 if y % 2 else y - 1
            return to if 0 <= to < count_y else None

        def around(x, y):
            return (x, round_y[(round_y.index(y) + 1) % count_y])

        def out_partner(x, y):
            return None if outward_x(x) is None else (outward_x(x), y)

        def b_partner(x, y):
            return None if side_b(y) is None else (x, side_b(y))

        def ring(x, y, up):
            to = x + 2 if x % 2 == up else x - 2
            return (to, y) if 0 <= to < count_x else (x ^ 1, y)

        make = functools.partial(swaps, count_x, count_y)
        core = lambda x, y: (x ^ 1, y)
        self.core = make(core, None)
        self.out_x = make(out_partner, around)
        self.side_a = make(lambda x, y: (x, y ^ 1), None)
        self.side_b = make(b_partner, core)
        self.ring_1 = make(lambda x, y: ring(x, y, 1), None)
        self.ring_0 = make(lambda x, y: ring(x, y, 0), None)


def depths(margin):
    return (margin, margin, margin, margin - 1, margin, margin, margin - 1)


def edge_tile(low, first, second, upper):
    up = upper == 1
    first = jnp.where(up, pltpu.roll(first, SUB // 2, 0), first)
    second = jnp.where(up, second, pltpu.roll(second, SUB // 2, 0))
    return jnp.where(low, first, second)


def tail_tile(low, odd, from_a, from_b, upper):
    after = jnp.where(odd == 0, from_a, from_b)
    before = jnp.where(odd == 0, from_b, from_a)
    if upper:
        after = pltpu.roll(after, SUB // 2, 0)
    else:
        before = pltpu.roll(before, SUB // 2, 0)
    return jnp.where(low, after, before)


def low_half(lanes):
    return lax.broadcasted_iota(jnp.int32, (SUB, lanes), 0) < SUB // 2


def position():
    at_x, at_y = lax.axis_index("gx"), lax.axis_index("gy")
    return at_x, at_y, lax.rem(at_x, 2), lax.rem(at_y, 2)


def pack_y(margin, fields, perm, ext, side_a, side_b, sems):
    width, rows, lanes = perm.shape
    _, _, _, odd = position()
    low = low_half(lanes)
    own = (pl.ds(margin, width), pl.ds(0, rows))
    loads = [pltpu.make_async_copy(fields.at[k] if k < 6 else perm, ext.at[(k, *own)], sems.at[k]) for k in range(7)]
    for load in loads:
        load.start()
    for k in range(7):
        loads[k].wait()

        def edge(x, upper):
            where = pl.ds(pl.multiple_of(upper * (rows - SUB), SUB), SUB)
            return edge_tile(low, ext[k, margin + x, where], ext[k, margin + x + width // 2, where], upper)

        for j in range(width // 2):
            side_a[k, j] = edge(j, 1 - odd)
            side_b[k, j] = edge(j, odd)


def pack_x(margin, ext, out_x, in_x):
    width, rows = ext.shape[1] - 2 * margin, ext.shape[2] - SUB
    _, _, core, _ = position()
    at = 0
    for k, depth in enumerate(depths(margin)):
        for j in range(depth):
            out_x[at + j] = ext[k, margin + core * (width - depth) + j, 0:rows]
            in_x[at + j] = ext[k, margin + (1 - core) * (width - depth) + j, 0:rows]
        at += depth


def valid_rows(low, at_y, count_y):
    return jnp.where(low, jnp.where(at_y < count_y - 1, 1, 0), jnp.where(at_y > 0, 1, 0)) > 0


def has_outward(at_x, core, count_x):
    return jnp.where(core == 0, at_x > 0, at_x < count_x - 1)


def join_y(margin, count_y, ext_in, side_a, side_b, ext, outer):
    del ext_in
    width, rows, lanes = ext.shape[1] - 2 * margin, ext.shape[2] - SUB, ext.shape[3]
    _, at_y, core, odd = position()
    low = low_half(lanes)
    valid = valid_rows(low, at_y, count_y)
    for k in range(7):
        for x in range(width):
            j, upper = x % (width // 2), x // (width // 2)
            tile = tail_tile(low, odd, side_a[k, j], side_b[k, j], upper)
            ext[k, margin + x, rows:] = jnp.where(valid, tile, 1.0 if k == 6 else 0.0)
        for j in range(margin):
            outer[k, j] = ext[k, margin + core * (width - margin) + j, rows:]


def join_inner(margin, count_y, ext_in, ext, inner):
    del ext_in
    width, rows, lanes = ext.shape[1] - 2 * margin, ext.shape[2] - SUB, ext.shape[3]
    _, at_y, core, _ = position()
    valid = valid_rows(low_half(lanes), at_y, count_y)
    for k in range(7):
        for j in range(margin):
            inner[k, j] = ext[k, margin + (1 - core) * (width - margin) + j, rows:]
    scale = COURANT * COURANT
    for x in range(margin, margin + width):
        ext[6, x, 0:rows] = scale / ext[6, x, 0:rows]
        ext[6, x, rows:] = jnp.where(valid, scale / ext[6, x, rows:], 0.0)


def load_rest(ext_in, forward, mask, offsets, taps, ext, forward_out, mask_out, weights, table, sems):
    del ext_in, ext
    lists = [pltpu.make_async_copy(offsets, table[0], sems.at[0]), pltpu.make_async_copy(taps, table[1], sems.at[1])]
    loads = [pltpu.make_async_copy(forward, forward_out, sems.at[2]), pltpu.make_async_copy(mask, mask_out, sems.at[3])]
    for load in lists + loads:
        load.start()
    for load in lists:
        load.wait()
    distance = lax.broadcasted_iota(jnp.int32, weights.shape, 0) - weights.shape[0] // 2
    total = jnp.zeros(weights.shape, jnp.float32)
    for b in range(offsets.shape[0]):
        total = total + jnp.where(distance == table[0][b], table[1][b], 0.0)
    weights[...] = total
    for load in loads:
        load.wait()


def join_core(margin, ext_in, in_x, ext):
    del ext_in
    width, rows = ext.shape[1] - 2 * margin, ext.shape[2] - SUB
    _, _, core, _ = position()
    in_at = (1 - core) * (width + margin)
    at = 0
    for k, depth in enumerate(depths(margin)):
        for j in range(depth):
            plane = in_x[at + j]
            plane = COURANT * COURANT / plane if k == 6 else plane
            ext[k, in_at + core * (margin - depth) + j, 0:rows] = plane
        at += depth


def join_outer(margin, count_x, ext_in, out_x, ext):
    del ext_in
    width, rows = ext.shape[1] - 2 * margin, ext.shape[2] - SUB
    at_x, _, core, _ = position()
    has_out = has_outward(at_x, core, count_x)
    out_at = core * (width + margin)
    at = 0
    for k, depth in enumerate(depths(margin)):
        for j in range(depth):
            plane = out_x[at + j]
            plane = COURANT * COURANT / plane if k == 6 else plane
            ext[k, out_at + (1 - core) * (margin - depth) + j, 0:rows] = jnp.where(has_out, plane, 0.0)
        at += depth


def join_corner(margin, count_x, count_y, ext_in, outer, ext):
    del ext_in
    width, rows, lanes = ext.shape[1] - 2 * margin, ext.shape[2] - SUB, ext.shape[3]
    at_x, at_y, core, _ = position()
    has_out = has_outward(at_x, core, count_x)
    valid = valid_rows(low_half(lanes), at_y, count_y) & jnp.broadcast_to(has_out, (SUB, lanes))
    out_at = core * (width + margin)
    for k in range(7):
        for j in range(margin):
            tile = outer[k, j]
            tile = jnp.where(valid, COURANT * COURANT / tile, 0.0) if k == 6 else jnp.where(has_out, tile, 0.0)
            ext[k, out_at + j, rows:] = tile


def steps(margin, ranges, ext, forward, mask, masked, final):
    width, rows, lanes = mask.shape
    high = rows + SUB
    at_x, at_y, _, _ = position()
    low = low_half(lanes)
    lane = lax.broadcasted_iota(jnp.int32, (high, lanes), 1)
    first_lane = lane == 0
    before_rows = jnp.where(low | jnp.broadcast_to(at_y > 0, (SUB, lanes)), 1.0, 0.0)
    before_x = jnp.where(at_x > 0, 1.0, 0.0)

    gap = lax.broadcasted_iota(jnp.int32, (lanes, lanes), 0) - lax.broadcasted_iota(jnp.int32, (lanes, lanes), 1)
    ahead = jnp.where(gap == 1, 1.0, 0.0) - jnp.where(gap == 0, 1.0, 0.0)
    ahead = jnp.concatenate([ahead, ahead], 0).astype(jnp.bfloat16)

    def ahead_z(k, first, end):
        f = ext[k, first:end].reshape((end - first) * high, lanes)
        main = f.astype(jnp.bfloat16)
        rest = (f - main.astype(jnp.float32)).astype(jnp.bfloat16)
        return jnp.dot(jnp.concatenate([main, rest], 1), ahead, preferred_element_type=jnp.float32)

    def next_y(f):
        return pltpu.roll(f, high - 1, 0)

    def last_y(f):
        return pltpu.roll(f, 1, 0)

    def last_z(f):
        return jnp.where(first_lane, 0.0, pltpu.roll(f, 1, 1))

    for turn, (first, first_e, end_h, end_e) in enumerate(ranges):
        last = turn == margin - 1
        ahead_x, ahead_y = ahead_z(0, first, end_h), ahead_z(1, first, end_h)
        held_y = held_z = None
        for i in range(first, end_e):
            ex, ey, ez = ext[0, i], ext[1, i], ext[2, i]
            hx, hy, hz = ext[3, i], ext[4, i], ext[5, i]
            if i < end_h:
                ey_x, ez_x = ext[1, i + 1], ext[2, i + 1]
                if turn == 0:
                    hx, hy, hz = hx * (1 / COURANT), hy * (1 / COURANT), hz * (1 / COURANT)
                here = slice((i - first) * high, (i - first + 1) * high)
                hx = hx - ((next_y(ez) - ez) - ahead_y[here])
                hy = hy - (ahead_x[here] - (ez_x - ez))
                hz = hz - ((ey_x - ey) - (next_y(ex) - ex))

                def clear(h):
                    h = jnp.concatenate([h[:rows], h[rows:] * before_rows], 0)
                    return h * before_x if i < margin else h

                hx, hy, hz = clear(hx), clear(hy), clear(hz)
                ext[3, i], ext[4, i], ext[5, i] = hx, hy, hz
            if i >= first_e:
                if held_y is None:
                    held_y, held_z = ext[4, i - 1], ext[5, i - 1]
                c = ext[6, i]
                ex = ex + c * ((hz - last_y(hz)) - (hy - last_z(hy)))
                ey = ey + c * ((hx - last_z(hx)) - (hz - held_z))
                ez = ez + c * ((hy - held_y) - (hx - last_y(hx)))
                if not last:
                    ext[0, i], ext[1, i], ext[2, i] = ex, ey, ez
                if margin <= i < margin + width:
                    x = i - margin
                    own_e = (ex[:rows], ey[:rows], ez[:rows])
                    total = sum(forward[turn, a, x].astype(jnp.float32) * own_e[a] for a in range(3))
                    if turn > 0:
                        total = total + masked[x]
                    if last:
                        total = total * mask[x].astype(jnp.float32)
                        for a in range(3):
                            final[a, x] = own_e[a]
                    masked[x] = total
            held_y, held_z = hy, hz


def inner_ranges(margin, width, core):
    top = width + 2 * margin - 1
    if core == 1:
        return [(t, t + 1, top - margin - t, top - margin - t) for t in range(margin)]
    return [(margin + t, margin + t + 1, top - t, top - t) for t in range(margin)]


def outer_ranges(margin, width, core):
    top = width + 2 * margin - 1
    if core == 1:
        return [(top - margin - t, top - margin - t, top - t, top - t) for t in range(margin)]
    return [(t, t + 1, margin + t, margin + t + 1) for t in range(margin)]


def early_steps(margin, count_y, ext_in, forward, mask, inner, ext, masked, final):
    del ext_in
    width, lanes = mask.shape[0], mask.shape[2]
    rows = mask.shape[1]
    _, at_y, core, _ = position()
    valid = valid_rows(low_half(lanes), at_y, count_y)
    in_at = (1 - core) * (width + margin)
    for k in range(7):
        for j in range(margin):
            tile = inner[k, j]
            ext[k, in_at + j, rows:] = jnp.where(valid, COURANT * COURANT / tile, 0.0) if k == 6 else tile
    for c in range(2):
        @pl.when(core == c)
        def _():
            steps(margin, inner_ranges(margin, width, c), ext, forward, mask, masked, final)


def late_steps(margin, ext_in, masked_in, final_in, forward, mask, ext, masked, final):
    del ext_in, masked_in, final_in
    _, _, core, _ = position()
    for c in range(2):
        @pl.when(core == c)
        def _():
            steps(margin, outer_ranges(margin, mask.shape[0], c), ext, forward, mask, masked, final)


def band_sum(reach, hop, sign, alone, weights, own, other, where, sums):
    width, _, lanes = own.shape
    _, _, core, _ = position()
    middle = weights.shape[0] // 2
    for j in range(width):
        for same in (True,) if alone else (True, False):
            plane = (own if same else other)[j, where]
            for x in range(width):
                distances = [j - x - 2 * hop * s * width + (0 if same else t * width) for s in (1, -1) for t in (1, -1)]
                if min(abs(distance) for distance in distances) > reach:
                    continue
                distance = j - x - 2 * hop * width * sign + (0 if same else (1 - 2 * core) * width)
                weight = jnp.broadcast_to(weights[pl.ds(middle + distance, 1)], (SUB, lanes))
                sums[x] = sums[x] + weight * plane
    return sums


def arrived(count_x, via_1, via_0, x, where):
    at_x, _, core, _ = position()
    first, second = via_1[x, where], via_0[x, where]
    up = core == 1
    before = jnp.where(at_x >= 2, jnp.where(up, first, second), 0.0)
    after = jnp.where(at_x < count_x - 2, jnp.where(up, second, first), 0.0)
    return before, after


def band_hop(reach, hop, count_x, up, alone, weights, own, *refs):
    *refs, send = refs
    other, via = (own, refs) if alone else (refs[0], refs[1:])
    width, rows, lanes = own.shape
    _, _, core, _ = position()
    ahead = core == up
    for r in range(rows // SUB):
        where = slice(r * SUB, (r + 1) * SUB)
        if via:
            start = [jnp.where(ahead, *arrived(count_x, *via, x, where)) for x in range(width)]
        else:
            start = [jnp.zeros((SUB, lanes), jnp.float32)] * width
        sums = band_sum(reach, hop, jnp.where(ahead, 1, -1), alone, weights, own, other, where, start)
        for x in range(width):
            send[x, where] = sums[x]


def band_own(reach, weights, own, other, final, base, stored, sem):
    store = pltpu.make_async_copy(final, stored, sem)
    store.start()
    width, rows, lanes = own.shape
    for r in range(rows // SUB):
        where = slice(r * SUB, (r + 1) * SUB)
        sums = band_sum(reach, 0, 1, False, weights, own, other, where, [jnp.zeros((SUB, lanes), jnp.float32)] * width)
        for x in range(width):
            base[x, where] = sums[x]
    store.wait()


def band_end(count_x, base, via_1, via_0, out):
    for x in range(out.shape[0]):
        before, after = arrived(count_x, via_1, via_0, x, slice(None))
        out[x] = base[x] + before + after


def shards(routes, adjoint_fields, forward_e, permittivity, design_mask, band_offsets, filter_taps):
    width, rows, lanes = permittivity.shape
    margin = ITERS
    f32 = jnp.float32
    planes = sum(depths(margin))
    shape = jax.ShapeDtypeStruct
    vmem = pl.BlockSpec(memory_space=pltpu.VMEM)
    hbm = pl.BlockSpec(memory_space=pltpu.HBM)
    params = pltpu.CompilerParams(vmem_limit_bytes=24 * 1024 * 1024)
    block = shape((width, rows, lanes), f32)
    ext = shape((7, width + 2 * margin, rows + SUB, lanes), f32)
    strip = shape((planes, rows, lanes), f32)
    edge = shape((7, width // 2, SUB, lanes), f32)
    corner = shape((7, margin, SUB, lanes), f32)
    reach = width * routes.count_x // 4
    rounds = -(-reach // (2 * width))
    distances = shape((4 * (rounds + 1) * width, lanes), f32)

    def cost(microseconds):
        return pl.CostEstimate(flops=int(microseconds * 1e9), bytes_accessed=int(microseconds * 3.6e6), transcendentals=0)

    def move(value, pairs):
        return lax.ppermute(value, BOTH, pairs)

    def from_hbm(*values):
        return [pltpu.with_memory_space_constraint(value, pltpu.HBM) for value in values]

    cells, side_a, side_b = pl.pallas_call(
        functools.partial(pack_y, margin),
        out_shape=(ext, edge, edge),
        in_specs=[hbm] * 2,
        out_specs=(vmem,) * 3,
        scratch_shapes=[pltpu.SemaphoreType.DMA((7,))],
        compiler_params=params,
        name="pack_y",
    )(*from_hbm(adjoint_fields, permittivity))
    out_x, in_x = pl.pallas_call(
        functools.partial(pack_x, margin),
        out_shape=(strip, strip),
        in_specs=[vmem],
        out_specs=(vmem,) * 2,
        compiler_params=params,
        name="pack_x",
    )(cells)
    side_b = move(side_b, routes.side_b)
    side_a = move(side_a, routes.side_a)
    in_x = move(in_x, routes.core)
    out_x = move(out_x, routes.out_x)
    cells, forward_e, design_mask, weights = pl.pallas_call(
        load_rest,
        out_shape=(ext, pltpu.VMEM(forward_e.shape, forward_e.dtype), pltpu.VMEM(design_mask.shape, design_mask.dtype), distances),
        in_specs=[vmem] + [hbm] * 4,
        out_specs=(vmem,) * 4,
        input_output_aliases={0: 0},
        scratch_shapes=[
            (pltpu.SMEM(band_offsets.shape, band_offsets.dtype), pltpu.SMEM(filter_taps.shape, filter_taps.dtype)),
            pltpu.SemaphoreType.DMA((4,)),
        ],
        compiler_params=params,
        cost_estimate=cost(JOIN_X_US),
        name="load_rest",
    )(cells, *from_hbm(forward_e, design_mask, band_offsets, filter_taps))
    cells, outer = pl.pallas_call(
        functools.partial(join_y, margin, routes.count_y),
        out_shape=(ext, corner),
        in_specs=[vmem] * 3,
        out_specs=(vmem,) * 2,
        input_output_aliases={0: 0},
        compiler_params=params,
        cost_estimate=cost(JOIN_Y_US),
        name="join_y",
    )(cells, side_a, side_b)
    outer = move(outer, routes.out_x)
    cells, inner = pl.pallas_call(
        functools.partial(join_inner, margin, routes.count_y),
        out_shape=(ext, corner),
        in_specs=[vmem],
        out_specs=(vmem,) * 2,
        input_output_aliases={0: 0},
        compiler_params=params,
        cost_estimate=cost(JOIN_X_US),
        name="join_inner",
    )(cells)
    inner = move(inner, routes.core)
    cells = pl.pallas_call(
        functools.partial(join_core, margin),
        out_shape=ext,
        in_specs=[vmem] * 2,
        out_specs=vmem,
        input_output_aliases={0: 0},
        compiler_params=params,
        cost_estimate=cost(JOIN_X_US),
        name="join_core",
    )(cells, in_x)
    fields = pltpu.VMEM((3, width, rows, lanes), f32)
    cells, masked, final = pl.pallas_call(
        functools.partial(early_steps, margin, routes.count_y),
        out_shape=(ext, block, fields),
        in_specs=[vmem] * 4,
        out_specs=(vmem,) * 3,
        input_output_aliases={0: 0},
        compiler_params=params,
        cost_estimate=cost(JOIN_X_US),
        name="early_steps",
    )(cells, forward_e, design_mask, inner)
    cells = pl.pallas_call(
        functools.partial(join_outer, margin, routes.count_x),
        out_shape=ext,
        in_specs=[vmem] * 2,
        out_specs=vmem,
        input_output_aliases={0: 0},
        compiler_params=params,
        cost_estimate=cost(JOIN_X_US),
        name="join_outer",
    )(cells, out_x)
    cells = pl.pallas_call(
        functools.partial(join_corner, margin, routes.count_x, routes.count_y),
        out_shape=ext,
        in_specs=[vmem] * 2,
        out_specs=vmem,
        input_output_aliases={0: 0},
        compiler_params=params,
        cost_estimate=cost(JOIN_X_US),
        name="join_corner",
    )(cells, outer)
    _, masked, final = pl.pallas_call(
        functools.partial(late_steps, margin),
        out_shape=(ext, block, fields),
        in_specs=[vmem] * 5,
        out_specs=(vmem,) * 3,
        input_output_aliases={0: 0, 1: 1, 2: 2},
        compiler_params=params,
        cost_estimate=cost(JOIN_X_US),
        name="late_steps",
    )(cells, masked, final, forward_e, design_mask)

    other = move(masked, routes.core)
    via = []

    def hop_kernel(hop, up, alone):
        operands = [weights, masked] + ([] if alone else [other]) + via
        return pl.pallas_call(
            functools.partial(band_hop, reach, hop, routes.count_x, up, alone),
            out_shape=block,
            in_specs=[vmem] * len(operands),
            out_specs=vmem,
            compiler_params=params,
            name="band_hop",
        )(*operands)

    for hop in range(rounds, 0, -1):
        send_1 = hop_kernel(hop, 1, hop == rounds)
        send_0 = hop_kernel(hop, 0, False)
        via = [move(send_1, routes.ring_1), move(send_0, routes.ring_0)]
    base, final = pl.pallas_call(
        functools.partial(band_own, reach),
        out_shape=(block, shape(final.shape, f32)),
        in_specs=[vmem] * 4,
        out_specs=(vmem, hbm),
        scratch_shapes=[pltpu.SemaphoreType.DMA],
        compiler_params=params,
        cost_estimate=cost(BAND_OWN_US),
        name="band_own",
    )(weights, masked, other, final)
    filtered = pl.pallas_call(
        functools.partial(band_end, routes.count_x),
        out_shape=block,
        in_specs=[vmem] * 3,
        out_specs=vmem,
        compiler_params=params,
        name="band_end",
    )(base, *via)
    return filtered, final


def solution(mesh):
    routes = Routes(mesh.shape["gx"], mesh.shape["gy"])
    return jax.shard_map(
        functools.partial(shards, routes),
        mesh=mesh,
        in_specs=(
            P(None, "gx", "gy", None),
            P(None, None, "gx", "gy", None),
            P("gx", "gy", None),
            P("gx", "gy", None),
            P(),
            P(),
        ),
        out_specs=(P("gx", "gy", None), P(None, "gx", "gy", None)),
        check_vma=False,
    )
```

```python
import functools
import jax
import jax.numpy as jnp
from jax import lax
from jax.experimental import pallas as pl
from jax.experimental.pallas import tpu as pltpu
from jax.sharding import PartitionSpec as P

ITERS = 4
COURANT = 0.5
BOTH = ("gx", "gy")
SUB = 8
JOIN_Y_US = 50
JOIN_X_US = 0.05
BAND_OWN_US = 2


def swaps(count_x, count_y, partner, idle):
    pairs = []
    for x in range(count_x):
        for y in range(count_y):
            to = partner(x, y)
            if to is None:
                to = idle(x, y)
            pairs.append((x * count_y + y, to[0] * count_y + to[1]))
    assert sorted(b for _, b in pairs) == sorted(a for a, _ in pairs)
    return pairs


class Routes:
    def __init__(self, count_x, count_y):
        self.count_x, self.count_y = count_x, count_y
        round_y = [y ^ (y >> 1) for y in range(count_y)]
        if sorted(round_y) != list(range(count_y)):
            round_y = list(range(count_y))

        def outward_x(x):
            to = x + 1 if x % 2 else x - 1
            return to if 0 <= to < count_x else None

        def side_b(y):
            to = y + 1 if y % 2 else y - 1
            return to if 0 <= to < count_y else None

        def around(x, y):
            return (x, round_y[(round_y.index(y) + 1) % count_y])

        def out_partner(x, y):
            return None if outward_x(x) is None else (outward_x(x), y)

        def b_partner(x, y):
            return None if side_b(y) is None else (x, side_b(y))

        def ring(x, y, up):
            to = x + 2 if x % 2 == up else x - 2
            return (to, y) if 0 <= to < count_x else (x ^ 1, y)

        make = functools.partial(swaps, count_x, count_y)
        core = lambda x, y: (x ^ 1, y)
        self.core = make(core, None)
        self.out_x = make(out_partner, around)
        self.side_a = [make(lambda x, y: (x, y ^ 1) if y // 2 % 2 == n else None, core) for n in range(2)]
        self.side_b = make(b_partner, core)
        self.ring_1 = make(lambda x, y: ring(x, y, 1), None)
        self.ring_0 = make(lambda x, y: ring(x, y, 0), None)


def depths(margin):
    return (margin, margin, margin, margin - 1, margin, margin, margin - 1)


def edge_tile(low, first, second, upper):
    up = upper == 1
    first = jnp.where(up, pltpu.roll(first, SUB // 2, 0), first)
    second = jnp.where(up, second, pltpu.roll(second, SUB // 2, 0))
    return jnp.where(low, first, second)


def tail_tile(low, odd, from_a, from_b, upper):
    after = jnp.where(odd == 0, from_a, from_b)
    before = jnp.where(odd == 0, from_b, from_a)
    if upper:
        after = pltpu.roll(after, SUB // 2, 0)
    else:
        before = pltpu.roll(before, SUB // 2, 0)
    return jnp.where(low, after, before)


def low_half(lanes):
    return lax.broadcasted_iota(jnp.int32, (SUB, lanes), 0) < SUB // 2


def position():
    at_x, at_y = lax.axis_index("gx"), lax.axis_index("gy")
    return at_x, at_y, lax.rem(at_x, 2), lax.rem(at_y, 2)


def pack_y(margin, fields, perm, ext, side_a0, side_b, side_a1, sems):
    width, rows, lanes = perm.shape
    _, _, _, odd = position()
    low = low_half(lanes)
    own = (pl.ds(margin, width), pl.ds(0, rows))
    loads = [pltpu.make_async_copy(fields.at[k] if k < 6 else perm, ext.at[(k, *own)], sems.at[k]) for k in range(7)]
    for load in loads:
        load.start()
    for k in range(7):
        loads[k].wait()

        def edge(x, upper):
            where = pl.ds(pl.multiple_of(upper * (rows - SUB), SUB), SUB)
            return edge_tile(low, ext[k, margin + x, where], ext[k, margin + x + width // 2, where], upper)

        for j in range(width // 2):
            side_a0[k, j] = side_a1[k, j] = edge(j, 1 - odd)
            side_b[k, j] = edge(j, odd)


def pack_x(margin, ext, out_x, in_x):
    width, rows = ext.shape[1] - 2 * margin, ext.shape[2] - SUB
    _, _, core, _ = position()
    at = 0
    for k, depth in enumerate(depths(margin)):
        for j in range(depth):
            out_x[at + j] = ext[k, margin + core * (width - depth) + j, 0:rows]
            in_x[at + j] = ext[k, margin + (1 - core) * (width - depth) + j, 0:rows]
        at += depth


def valid_rows(low, at_y, count_y):
    return jnp.where(low, jnp.where(at_y < count_y - 1, 1, 0), jnp.where(at_y > 0, 1, 0)) > 0


def has_outward(at_x, core, count_x):
    return jnp.where(core == 0, at_x > 0, at_x < count_x - 1)


def join_y(margin, count_y, ext_in, side_a0, side_b, side_a1, ext, outer):
    del ext_in
    width, rows, lanes = ext.shape[1] - 2 * margin, ext.shape[2] - SUB, ext.shape[3]
    _, at_y, core, odd = position()
    low = low_half(lanes)
    valid = valid_rows(low, at_y, count_y)
    in_first = lax.rem(at_y // 2, 2) == 0
    for k in range(7):
        for x in range(width):
            j, upper = x % (width // 2), x // (width // 2)
            side_a = jnp.where(in_first, side_a0[k, j], side_a1[k, j])
            tile = tail_tile(low, odd, side_a, side_b[k, j], upper)
            ext[k, margin + x, rows:] = jnp.where(valid, tile, 1.0 if k == 6 else 0.0)
        for j in range(margin):
            outer[k, j] = ext[k, margin + core * (width - margin) + j, rows:]


def join_inner(margin, count_y, ext_in, ext, inner):
    del ext_in
    width, rows, lanes = ext.shape[1] - 2 * margin, ext.shape[2] - SUB, ext.shape[3]
    _, at_y, core, _ = position()
    valid = valid_rows(low_half(lanes), at_y, count_y)
    for k in range(7):
        for j in range(margin):
            inner[k, j] = ext[k, margin + (1 - core) * (width - margin) + j, rows:]
    scale = COURANT * COURANT
    for x in range(margin, margin + width):
        ext[6, x, 0:rows] = scale / ext[6, x, 0:rows]
        ext[6, x, rows:] = jnp.where(valid, scale / ext[6, x, rows:], 0.0)


def load_rest(ext_in, forward, mask, offsets, taps, ext, forward_out, mask_out, weights, table, sems):
    del ext_in, ext
    lists = [pltpu.make_async_copy(offsets, table[0], sems.at[0]), pltpu.make_async_copy(taps, table[1], sems.at[1])]
    loads = [pltpu.make_async_copy(forward, forward_out, sems.at[2]), pltpu.make_async_copy(mask, mask_out, sems.at[3])]
    for load in lists + loads:
        load.start()
    for load in lists:
        load.wait()
    distance = lax.broadcasted_iota(jnp.int32, weights.shape, 0) - weights.shape[0] // 2
    total = jnp.zeros(weights.shape, jnp.float32)
    for b in range(offsets.shape[0]):
        total = total + jnp.where(distance == table[0][b], table[1][b], 0.0)
    weights[...] = total
    for load in loads:
        load.wait()


def join_core(margin, ext_in, in_x, ext):
    del ext_in
    width, rows = ext.shape[1] - 2 * margin, ext.shape[2] - SUB
    _, _, core, _ = position()
    in_at = (1 - core) * (width + margin)
    at = 0
    for k, depth in enumerate(depths(margin)):
        for j in range(depth):
            plane = in_x[at + j]
            plane = COURANT * COURANT / plane if k == 6 else plane
            ext[k, in_at + core * (margin - depth) + j, 0:rows] = plane
        at += depth


def join_outer(margin, count_x, ext_in, out_x, ext):
    del ext_in
    width, rows = ext.shape[1] - 2 * margin, ext.shape[2] - SUB
    at_x, _, core, _ = position()
    has_out = has_outward(at_x, core, count_x)
    out_at = core * (width + margin)
    at = 0
    for k, depth in enumerate(depths(margin)):
        for j in range(depth):
            plane = out_x[at + j]
            plane = COURANT * COURANT / plane if k == 6 else plane
            ext[k, out_at + (1 - core) * (margin - depth) + j, 0:rows] = jnp.where(has_out, plane, 0.0)
        at += depth


def join_corner(margin, count_x, count_y, ext_in, outer, ext):
    del ext_in
    width, rows, lanes = ext.shape[1] - 2 * margin, ext.shape[2] - SUB, ext.shape[3]
    at_x, at_y, core, _ = position()
    has_out = has_outward(at_x, core, count_x)
    valid = valid_rows(low_half(lanes), at_y, count_y) & jnp.broadcast_to(has_out, (SUB, lanes))
    out_at = core * (width + margin)
    for k in range(7):
        for j in range(margin):
            tile = outer[k, j]
            tile = jnp.where(valid, COURANT * COURANT / tile, 0.0) if k == 6 else jnp.where(has_out, tile, 0.0)
            ext[k, out_at + j, rows:] = tile


def steps(margin, ranges, ext, forward, mask, masked, final):
    width, rows, lanes = mask.shape
    high = rows + SUB
    at_x, at_y, _, _ = position()
    low = low_half(lanes)
    lane = lax.broadcasted_iota(jnp.int32, (high, lanes), 1)
    first_lane = lane == 0
    before_rows = jnp.where(low | jnp.broadcast_to(at_y > 0, (SUB, lanes)), 1.0, 0.0)
    before_x = jnp.where(at_x > 0, 1.0, 0.0)

    gap = lax.broadcasted_iota(jnp.int32, (lanes, lanes), 0) - lax.broadcasted_iota(jnp.int32, (lanes, lanes), 1)
    ahead = jnp.where(gap == 1, 1.0, 0.0) - jnp.where(gap == 0, 1.0, 0.0)
    ahead = jnp.concatenate([ahead, ahead], 0).astype(jnp.bfloat16)

    def ahead_z(k, first, end):
        f = ext[k, first:end].reshape((end - first) * high, lanes)
        main = f.astype(jnp.bfloat16)
        rest = (f - main.astype(jnp.float32)).astype(jnp.bfloat16)
        return jnp.dot(jnp.concatenate([main, rest], 1), ahead, preferred_element_type=jnp.float32)

    def next_y(f):
        return pltpu.roll(f, high - 1, 0)

    def last_y(f):
        return pltpu.roll(f, 1, 0)

    def last_z(f):
        return jnp.where(first_lane, 0.0, pltpu.roll(f, 1, 1))

    for turn, (first, first_e, end_h, end_e) in enumerate(ranges):
        last = turn == margin - 1
        ahead_x, ahead_y = ahead_z(0, first, end_h), ahead_z(1, first, end_h)
        held_y = held_z = None
        for i in range(first, end_e):
            ex, ey, ez = ext[0, i], ext[1, i], ext[2, i]
            hx, hy, hz = ext[3, i], ext[4, i], ext[5, i]
            if i < end_h:
                ey_x, ez_x = ext[1, i + 1], ext[2, i + 1]
                if turn == 0:
                    hx, hy, hz = hx * (1 / COURANT), hy * (1 / COURANT), hz * (1 / COURANT)
                here = slice((i - first) * high, (i - first + 1) * high)
                hx = hx - ((next_y(ez) - ez) - ahead_y[here])
                hy = hy - (ahead_x[here] - (ez_x - ez))
                hz = hz - ((ey_x - ey) - (next_y(ex) - ex))

                def clear(h):
                    h = jnp.concatenate([h[:rows], h[rows:] * before_rows], 0)
                    return h * before_x if i < margin else h

                hx, hy, hz = clear(hx), clear(hy), clear(hz)
                ext[3, i], ext[4, i], ext[5, i] = hx, hy, hz
            if i >= first_e:
                if held_y is None:
                    held_y, held_z = ext[4, i - 1], ext[5, i - 1]
                c = ext[6, i]
                ex = ex + c * ((hz - last_y(hz)) - (hy - last_z(hy)))
                ey = ey + c * ((hx - last_z(hx)) - (hz - held_z))
                ez = ez + c * ((hy - held_y) - (hx - last_y(hx)))
                if not last:
                    ext[0, i], ext[1, i], ext[2, i] = ex, ey, ez
                if margin <= i < margin + width:
                    x = i - margin
                    own_e = (ex[:rows], ey[:rows], ez[:rows])
                    total = sum(forward[turn, a, x].astype(jnp.float32) * own_e[a] for a in range(3))
                    if turn > 0:
                        total = total + masked[x]
                    if last:
                        total = total * mask[x].astype(jnp.float32)
                        for a in range(3):
                            final[a, x] = own_e[a]
                    masked[x] = total
            held_y, held_z = hy, hz


def inner_ranges(margin, width, core):
    top = width + 2 * margin - 1
    if core == 1:
        return [(t, t + 1, top - margin - t, top - margin - t) for t in range(margin)]
    return [(margin + t, margin + t + 1, top - t, top - t) for t in range(margin)]


def outer_ranges(margin, width, core):
    top = width + 2 * margin - 1
    if core == 1:
        return [(top - margin - t, top - margin - t, top - t, top - t) for t in range(margin)]
    return [(t, t + 1, margin + t, margin + t + 1) for t in range(margin)]


def early_steps(margin, count_y, ext_in, forward, mask, inner, ext, masked, final):
    del ext_in
    width, lanes = mask.shape[0], mask.shape[2]
    rows = mask.shape[1]
    _, at_y, core, _ = position()
    valid = valid_rows(low_half(lanes), at_y, count_y)
    in_at = (1 - core) * (width + margin)
    for k in range(7):
        for j in range(margin):
            tile = inner[k, j]
            ext[k, in_at + j, rows:] = jnp.where(valid, COURANT * COURANT / tile, 0.0) if k == 6 else tile
    for c in range(2):
        @pl.when(core == c)
        def _():
            steps(margin, inner_ranges(margin, width, c), ext, forward, mask, masked, final)


def late_steps(margin, ext_in, masked_in, final_in, forward, mask, ext, masked, final):
    del ext_in, masked_in, final_in
    _, _, core, _ = position()
    for c in range(2):
        @pl.when(core == c)
        def _():
            steps(margin, outer_ranges(margin, mask.shape[0], c), ext, forward, mask, masked, final)


def band_sum(reach, hop, sign, alone, weights, own, other, where, sums):
    width, _, lanes = own.shape
    _, _, core, _ = position()
    middle = weights.shape[0] // 2
    for j in range(width):
        for same in (True,) if alone else (True, False):
            plane = (own if same else other)[j, where]
            for x in range(width):
                distances = [j - x - 2 * hop * s * width + (0 if same else t * width) for s in (1, -1) for t in (1, -1)]
                if min(abs(distance) for distance in distances) > reach:
                    continue
                distance = j - x - 2 * hop * width * sign + (0 if same else (1 - 2 * core) * width)
                weight = jnp.broadcast_to(weights[pl.ds(middle + distance, 1)], (SUB, lanes))
                sums[x] = sums[x] + weight * plane
    return sums


def arrived(count_x, via_1, via_0, x, where):
    at_x, _, core, _ = position()
    first, second = via_1[x, where], via_0[x, where]
    up = core == 1
    before = jnp.where(at_x >= 2, jnp.where(up, first, second), 0.0)
    after = jnp.where(at_x < count_x - 2, jnp.where(up, second, first), 0.0)
    return before, after


def band_hop(reach, hop, count_x, up, alone, weights, own, *refs):
    *refs, send = refs
    other, via = (own, refs) if alone else (refs[0], refs[1:])
    width, rows, lanes = own.shape
    _, _, core, _ = position()
    ahead = core == up
    for r in range(rows // SUB):
        where = slice(r * SUB, (r + 1) * SUB)
        if via:
            start = [jnp.where(ahead, *arrived(count_x, *via, x, where)) for x in range(width)]
        else:
            start = [jnp.zeros((SUB, lanes), jnp.float32)] * width
        sums = band_sum(reach, hop, jnp.where(ahead, 1, -1), alone, weights, own, other, where, start)
        for x in range(width):
            send[x, where] = sums[x]


def band_own(reach, weights, own, other, final, base, stored, sem):
    store = pltpu.make_async_copy(final, stored, sem)
    store.start()
    width, rows, lanes = own.shape
    for r in range(rows // SUB):
        where = slice(r * SUB, (r + 1) * SUB)
        sums = band_sum(reach, 0, 1, False, weights, own, other, where, [jnp.zeros((SUB, lanes), jnp.float32)] * width)
        for x in range(width):
            base[x, where] = sums[x]
    store.wait()


def band_end(count_x, base, via_1, via_0, out):
    for x in range(out.shape[0]):
        before, after = arrived(count_x, via_1, via_0, x, slice(None))
        out[x] = base[x] + before + after


def shards(routes, adjoint_fields, forward_e, permittivity, design_mask, band_offsets, filter_taps):
    width, rows, lanes = permittivity.shape
    margin = ITERS
    f32 = jnp.float32
    planes = sum(depths(margin))
    shape = jax.ShapeDtypeStruct
    vmem = pl.BlockSpec(memory_space=pltpu.VMEM)
    hbm = pl.BlockSpec(memory_space=pltpu.HBM)
    params = pltpu.CompilerParams(vmem_limit_bytes=24 * 1024 * 1024)
    block = shape((width, rows, lanes), f32)
    ext = shape((7, width + 2 * margin, rows + SUB, lanes), f32)
    strip = shape((planes, rows, lanes), f32)
    edge = shape((7, width // 2, SUB, lanes), f32)
    corner = shape((7, margin, SUB, lanes), f32)
    reach = width * routes.count_x // 4
    rounds = -(-reach // (2 * width))
    distances = shape((4 * (rounds + 1) * width, lanes), f32)

    def cost(microseconds):
        return pl.CostEstimate(flops=int(microseconds * 1e9), bytes_accessed=int(microseconds * 3.6e6), transcendentals=0)

    def move(value, pairs):
        return lax.ppermute(value, BOTH, pairs)

    def from_hbm(*values):
        return [pltpu.with_memory_space_constraint(value, pltpu.HBM) for value in values]

    cells, side_a0, side_b, side_a1 = pl.pallas_call(
        functools.partial(pack_y, margin),
        out_shape=(ext, edge, edge, edge),
        in_specs=[hbm] * 2,
        out_specs=(vmem,) * 4,
        scratch_shapes=[pltpu.SemaphoreType.DMA((7,))],
        compiler_params=params,
        name="pack_y",
    )(*from_hbm(adjoint_fields, permittivity))
    out_x, in_x = pl.pallas_call(
        functools.partial(pack_x, margin),
        out_shape=(strip, strip),
        in_specs=[vmem],
        out_specs=(vmem,) * 2,
        compiler_params=params,
        name="pack_x",
    )(cells)
    side_a0 = move(side_a0, routes.side_a[0])
    side_b = move(side_b, routes.side_b)
    side_a1 = move(side_a1, routes.side_a[1])
    in_x = move(in_x, routes.core)
    out_x = move(out_x, routes.out_x)
    cells, forward_e, design_mask, weights = pl.pallas_call(
        load_rest,
        out_shape=(ext, pltpu.VMEM(forward_e.shape, forward_e.dtype), pltpu.VMEM(design_mask.shape, design_mask.dtype), distances),
        in_specs=[vmem] + [hbm] * 4,
        out_specs=(vmem,) * 4,
        input_output_aliases={0: 0},
        scratch_shapes=[
            (pltpu.SMEM(band_offsets.shape, band_offsets.dtype), pltpu.SMEM(filter_taps.shape, filter_taps.dtype)),
            pltpu.SemaphoreType.DMA((4,)),
        ],
        compiler_params=params,
        cost_estimate=cost(JOIN_X_US),
        name="load_rest",
    )(cells, *from_hbm(forward_e, design_mask, band_offsets, filter_taps))
    cells, outer = pl.pallas_call(
        functools.partial(join_y, margin, routes.count_y),
        out_shape=(ext, corner),
        in_specs=[vmem] * 4,
        out_specs=(vmem,) * 2,
        input_output_aliases={0: 0},
        compiler_params=params,
        cost_estimate=cost(JOIN_Y_US),
        name="join_y",
    )(cells, side_a0, side_b, side_a1)
    outer = move(outer, routes.out_x)
    cells, inner = pl.pallas_call(
        functools.partial(join_inner, margin, routes.count_y),
        out_shape=(ext, corner),
        in_specs=[vmem],
        out_specs=(vmem,) * 2,
        input_output_aliases={0: 0},
        compiler_params=params,
        cost_estimate=cost(JOIN_X_US),
        name="join_inner",
    )(cells)
    inner = move(inner, routes.core)
    cells = pl.pallas_call(
        functools.partial(join_core, margin),
        out_shape=ext,
        in_specs=[vmem] * 2,
        out_specs=vmem,
        input_output_aliases={0: 0},
        compiler_params=params,
        cost_estimate=cost(JOIN_X_US),
        name="join_core",
    )(cells, in_x)
    fields = pltpu.VMEM((3, width, rows, lanes), f32)
    cells, masked, final = pl.pallas_call(
        functools.partial(early_steps, margin, routes.count_y),
        out_shape=(ext, block, fields),
        in_specs=[vmem] * 4,
        out_specs=(vmem,) * 3,
        input_output_aliases={0: 0},
        compiler_params=params,
        cost_estimate=cost(JOIN_X_US),
        name="early_steps",
    )(cells, forward_e, design_mask, inner)
    cells = pl.pallas_call(
        functools.partial(join_outer, margin, routes.count_x),
        out_shape=ext,
        in_specs=[vmem] * 2,
        out_specs=vmem,
        input_output_aliases={0: 0},
        compiler_params=params,
        cost_estimate=cost(JOIN_X_US),
        name="join_outer",
    )(cells, out_x)
    cells = pl.pallas_call(
        functools.partial(join_corner, margin, routes.count_x, routes.count_y),
        out_shape=ext,
        in_specs=[vmem] * 2,
        out_specs=vmem,
        input_output_aliases={0: 0},
        compiler_params=params,
        cost_estimate=cost(JOIN_X_US),
        name="join_corner",
    )(cells, outer)
    _, masked, final = pl.pallas_call(
        functools.partial(late_steps, margin),
        out_shape=(ext, block, fields),
        in_specs=[vmem] * 5,
        out_specs=(vmem,) * 3,
        input_output_aliases={0: 0, 1: 1, 2: 2},
        compiler_params=params,
        cost_estimate=cost(JOIN_X_US),
        name="late_steps",
    )(cells, masked, final, forward_e, design_mask)

    other = move(masked, routes.core)
    via = []

    def hop_kernel(hop, up, alone):
        operands = [weights, masked] + ([] if alone else [other]) + via
        return pl.pallas_call(
            functools.partial(band_hop, reach, hop, routes.count_x, up, alone),
            out_shape=block,
            in_specs=[vmem] * len(operands),
            out_specs=vmem,
            compiler_params=params,
            name="band_hop",
        )(*operands)

    for hop in range(rounds, 0, -1):
        send_1 = hop_kernel(hop, 1, hop == rounds)
        send_0 = hop_kernel(hop, 0, False)
        via = [move(send_1, routes.ring_1), move(send_0, routes.ring_0)]
    base, final = pl.pallas_call(
        functools.partial(band_own, reach),
        out_shape=(block, shape(final.shape, f32)),
        in_specs=[vmem] * 4,
        out_specs=(vmem, hbm),
        scratch_shapes=[pltpu.SemaphoreType.DMA],
        compiler_params=params,
        cost_estimate=cost(BAND_OWN_US),
        name="band_own",
    )(weights, masked, other, final)
    filtered = pl.pallas_call(
        functools.partial(band_end, routes.count_x),
        out_shape=block,
        in_specs=[vmem] * 3,
        out_specs=vmem,
        compiler_params=params,
        name="band_end",
    )(base, *via)
    return filtered, final


def solution(mesh):
    routes = Routes(mesh.shape["gx"], mesh.shape["gy"])
    return jax.shard_map(
        functools.partial(shards, routes),
        mesh=mesh,
        in_specs=(
            P(None, "gx", "gy", None),
            P(None, None, "gx", "gy", None),
            P("gx", "gy", None),
            P("gx", "gy", None),
            P(),
            P(),
        ),
        out_specs=(P("gx", "gy", None), P(None, "gx", "gy", None)),
        check_vma=False,
    )
```

```python
import functools
import jax
import jax.numpy as jnp
from jax import lax
from jax.experimental import pallas as pl
from jax.experimental.pallas import tpu as pltpu
from jax.sharding import PartitionSpec as P

ITERS = 4
COURANT = 0.5
BOTH = ("gx", "gy")
SUB = 8
JOIN_Y_US = 50
JOIN_X_US = 0.05
BAND_OWN_US = 2


def swaps(count_x, count_y, partner, idle):
    pairs = []
    for x in range(count_x):
        for y in range(count_y):
            to = partner(x, y)
            if to is None:
                to = idle(x, y)
            pairs.append((x * count_y + y, to[0] * count_y + to[1]))
    assert sorted(b for _, b in pairs) == sorted(a for a, _ in pairs)
    return pairs


class Routes:
    def __init__(self, count_x, count_y):
        self.count_x, self.count_y = count_x, count_y
        round_y = [y ^ (y >> 1) for y in range(count_y)]
        if sorted(round_y) != list(range(count_y)):
            round_y = list(range(count_y))

        def outward_x(x):
            to = x + 1 if x % 2 else x - 1
            return to if 0 <= to < count_x else None

        def side_b(y):
            to = y + 1 if y % 2 else y - 1
            return to if 0 <= to < count_y else None

        def around(x, y):
            return (x, round_y[(round_y.index(y) + 1) % count_y])

        def out_partner(x, y):
            return None if outward_x(x) is None else (outward_x(x), y)

        def b_partner(x, y):
            return None if side_b(y) is None else (x, side_b(y))

        def ring(x, y, up):
            to = x + 2 if x % 2 == up else x - 2
            return (to, y) if 0 <= to < count_x else (x ^ 1, y)

        make = functools.partial(swaps, count_x, count_y)
        core = lambda x, y: (x ^ 1, y)
        self.core = make(core, None)
        self.out_x = make(out_partner, around)
        self.side_a = [make(lambda x, y: (x, y ^ 1) if y // 2 % 2 == n else None, core) for n in range(2)]
        self.side_b = make(b_partner, core)
        self.ring_1 = make(lambda x, y: ring(x, y, 1), None)
        self.ring_0 = make(lambda x, y: ring(x, y, 0), None)


def depths(margin):
    return (margin, margin, margin, margin - 1, margin, margin, margin - 1)


def edge_tile(low, first, second, upper):
    up = upper == 1
    first = jnp.where(up, pltpu.roll(first, SUB // 2, 0), first)
    second = jnp.where(up, second, pltpu.roll(second, SUB // 2, 0))
    return jnp.where(low, first, second)


def tail_tile(low, odd, from_a, from_b, upper):
    after = jnp.where(odd == 0, from_a, from_b)
    before = jnp.where(odd == 0, from_b, from_a)
    if upper:
        after = pltpu.roll(after, SUB // 2, 0)
    else:
        before = pltpu.roll(before, SUB // 2, 0)
    return jnp.where(low, after, before)


SHORT = (4, 6)
LONG = (0, 1, 2, 3, 5)


def short_places(width, depth):
    for n, (k, x) in enumerate((k, x) for k in SHORT for x in range(width)):
        yield k, x, n * depth // SUB, n * depth % SUB


def side_tiles(width, margin):
    assert margin * 2 == SUB
    return len(LONG) * width // 2, -(-len(SHORT) * width * (margin - 1) // SUB)


def low_half(lanes):
    return lax.broadcasted_iota(jnp.int32, (SUB, lanes), 0) < SUB // 2


def position():
    at_x, at_y = lax.axis_index("gx"), lax.axis_index("gy")
    return at_x, at_y, lax.rem(at_x, 2), lax.rem(at_y, 2)


def pack_y(margin, fields, perm, ext, side_a0, side_b, side_a1, sems):
    width, rows, lanes = perm.shape
    _, _, _, odd = position()
    low = low_half(lanes)
    own = (pl.ds(margin, width), pl.ds(0, rows))
    loads = [pltpu.make_async_copy(fields.at[k] if k < 6 else perm, ext.at[(k, *own)], sems.at[k]) for k in range(7)]
    for load in loads:
        load.start()

    def rows_of(k, x, upper):
        return ext[k, margin + x, pl.ds(pl.multiple_of(upper * (rows - SUB), SUB), SUB)]

    for k in range(7):
        loads[k].wait()
        if k in LONG:
            for j in range(width // 2):
                for upper, to in ((1 - odd, (side_a0, side_a1)), (odd, (side_b,))):
                    tile = edge_tile(low, rows_of(k, j, upper), rows_of(k, j + width // 2, upper), upper)
                    for ref in to:
                        ref[LONG.index(k) * (width // 2) + j] = tile
    long_tiles, _ = side_tiles(width, margin)
    depth = margin - 1
    sub = lax.broadcasted_iota(jnp.int32, (SUB, lanes), 0)
    for upper, to in ((1 - odd, (side_a0, side_a1)), (odd, (side_b,))):
        tiles = {}
        for k, x, t, at in short_places(width, depth):
            rows_kx = rows_of(k, x, upper)
            rows_kx = jnp.where(upper == 1, pltpu.roll(rows_kx, depth, 0), rows_kx)
            rows_kx = pltpu.roll(rows_kx, at, 0) if at else rows_kx
            tiles[t] = jnp.where(sub >= at, rows_kx, tiles[t]) if t in tiles else rows_kx
            if at + depth > SUB:
                tiles[t + 1] = rows_kx
        for t, tile in tiles.items():
            for ref in to:
                ref[long_tiles + t] = tile


def pack_x(margin, ext, out_x, in_x):
    width, rows = ext.shape[1] - 2 * margin, ext.shape[2] - SUB
    _, _, core, _ = position()
    at = 0
    for k, depth in enumerate(depths(margin)):
        for j in range(depth):
            out_x[at + j] = ext[k, margin + core * (width - depth) + j, 0:rows]
            in_x[at + j] = ext[k, margin + (1 - core) * (width - depth) + j, 0:rows]
        at += depth


def valid_rows(low, at_y, count_y):
    return jnp.where(low, jnp.where(at_y < count_y - 1, 1, 0), jnp.where(at_y > 0, 1, 0)) > 0


def has_outward(at_x, core, count_x):
    return jnp.where(core == 0, at_x > 0, at_x < count_x - 1)


def join_y(margin, count_y, ext_in, side_a0, side_b, side_a1, ext, outer):
    del ext_in
    width, rows, lanes = ext.shape[1] - 2 * margin, ext.shape[2] - SUB, ext.shape[3]
    _, at_y, core, odd = position()
    low = low_half(lanes)
    has_after, has_before = at_y < count_y - 1, at_y > 0
    valid = valid_rows(low, at_y, count_y)
    in_first = lax.rem(at_y // 2, 2) == 0
    long_tiles, short_tiles = side_tiles(width, margin)
    depth = margin - 1
    sub = lax.broadcasted_iota(jnp.int32, (SUB, lanes), 0)

    def from_sides(t):
        side_a = jnp.where(in_first, side_a0[t], side_a1[t])
        return side_a, side_b[t]

    after, before = [], []
    for t in range(short_tiles):
        from_a, from_b = from_sides(long_tiles + t)
        after.append(jnp.where(odd == 0, from_a, from_b))
        before.append(jnp.where(odd == 0, from_b, from_a))

    def short_rows(tiles, t, at, to):
        tile = tiles[t]
        if at + depth > SUB:
            tile = jnp.where(sub >= at, tile, tiles[t + 1])
        return pltpu.roll(tile, (to - at) % SUB, 0) if (to - at) % SUB else tile

    for k, x, t, at in short_places(width, depth):
        blank = 1.0 if k == 6 else 0.0
        tile = jnp.where((sub < depth) & jnp.broadcast_to(has_after, (SUB, lanes)), short_rows(after, t, at, 0), blank)
        upper_rows = (sub >= SUB - depth) & jnp.broadcast_to(has_before, (SUB, lanes))
        ext[k, margin + x, rows:] = jnp.where(upper_rows, short_rows(before, t, at, SUB - depth), tile)
    for k in range(7):
        for x in range(width if k in LONG else 0):
            j, upper = x % (width // 2), x // (width // 2)
            tile = tail_tile(low, odd, *from_sides(LONG.index(k) * (width // 2) + j), upper)
            ext[k, margin + x, rows:] = jnp.where(valid, tile, 0.0)
        for j in range(margin):
            outer[k, j] = ext[k, margin + core * (width - margin) + j, rows:]


def join_inner(margin, count_y, ext_in, ext, inner):
    del ext_in
    width, rows, lanes = ext.shape[1] - 2 * margin, ext.shape[2] - SUB, ext.shape[3]
    _, at_y, core, _ = position()
    valid = valid_rows(low_half(lanes), at_y, count_y)
    for k in range(7):
        for j in range(margin):
            inner[k, j] = ext[k, margin + (1 - core) * (width - margin) + j, rows:]
    scale = COURANT * COURANT
    for x in range(margin, margin + width):
        ext[6, x, 0:rows] = scale / ext[6, x, 0:rows]
        ext[6, x, rows:] = jnp.where(valid, scale / ext[6, x, rows:], 0.0)


def load_rest(ext_in, forward, mask, offsets, taps, ext, forward_out, mask_out, weights, table, sems):
    del ext_in, ext
    lists = [pltpu.make_async_copy(offsets, table[0], sems.at[0]), pltpu.make_async_copy(taps, table[1], sems.at[1])]
    loads = [pltpu.make_async_copy(forward, forward_out, sems.at[2]), pltpu.make_async_copy(mask, mask_out, sems.at[3])]
    for load in lists + loads:
        load.start()
    for load in lists:
        load.wait()
    distance = lax.broadcasted_iota(jnp.int32, weights.shape, 0) - weights.shape[0] // 2
    total = jnp.zeros(weights.shape, jnp.float32)
    for b in range(offsets.shape[0]):
        total = total + jnp.where(distance == table[0][b], table[1][b], 0.0)
    weights[...] = total
    for load in loads:
        load.wait()


def join_core(margin, ext_in, in_x, ext):
    del ext_in
    width, rows = ext.shape[1] - 2 * margin, ext.shape[2] - SUB
    _, _, core, _ = position()
    in_at = (1 - core) * (width + margin)
    at = 0
    for k, depth in enumerate(depths(margin)):
        for j in range(depth):
            plane = in_x[at + j]
            plane = COURANT * COURANT / plane if k == 6 else plane
            ext[k, in_at + core * (margin - depth) + j, 0:rows] = plane
        at += depth


def join_outer(margin, count_x, ext_in, out_x, ext):
    del ext_in
    width, rows = ext.shape[1] - 2 * margin, ext.shape[2] - SUB
    at_x, _, core, _ = position()
    has_out = has_outward(at_x, core, count_x)
    out_at = core * (width + margin)
    at = 0
    for k, depth in enumerate(depths(margin)):
        for j in range(depth):
            plane = out_x[at + j]
            plane = COURANT * COURANT / plane if k == 6 else plane
            ext[k, out_at + (1 - core) * (margin - depth) + j, 0:rows] = jnp.where(has_out, plane, 0.0)
        at += depth


def join_corner(margin, count_x, count_y, ext_in, outer, ext):
    del ext_in
    width, rows, lanes = ext.shape[1] - 2 * margin, ext.shape[2] - SUB, ext.shape[3]
    at_x, at_y, core, _ = position()
    has_out = has_outward(at_x, core, count_x)
    valid = valid_rows(low_half(lanes), at_y, count_y) & jnp.broadcast_to(has_out, (SUB, lanes))
    out_at = core * (width + margin)
    for k in range(7):
        for j in range(margin):
            tile = outer[k, j]
            tile = jnp.where(valid, COURANT * COURANT / tile, 0.0) if k == 6 else jnp.where(has_out, tile, 0.0)
            ext[k, out_at + j, rows:] = tile


def steps(margin, ranges, product, ext, forward, mask, masked, final):
    width, rows, lanes = mask.shape
    high = rows + SUB
    at_x, at_y, _, _ = position()
    low = low_half(lanes)
    lane = lax.broadcasted_iota(jnp.int32, (high, lanes), 1)
    first_lane, last_lane = lane == 0, lane == lanes - 1
    before_rows = jnp.where(low | jnp.broadcast_to(at_y > 0, (SUB, lanes)), 1.0, 0.0)
    before_x = jnp.where(at_x > 0, 1.0, 0.0)

    gap = lax.broadcasted_iota(jnp.int32, (lanes, lanes), 0) - lax.broadcasted_iota(jnp.int32, (lanes, lanes), 1)
    ahead = jnp.where(gap == 1, 1.0, 0.0) - jnp.where(gap == 0, 1.0, 0.0)
    ahead = jnp.concatenate([ahead, ahead], 0).astype(jnp.bfloat16)

    def ahead_z(first, end):
        f = ext[0:2, first:end].reshape(2 * (end - first) * high, lanes)
        main = f.astype(jnp.bfloat16)
        rest = (f - main.astype(jnp.float32)).astype(jnp.bfloat16)
        return jnp.dot(jnp.concatenate([main, rest], 1), ahead, preferred_element_type=jnp.float32)

    def next_y(f):
        return pltpu.roll(f, high - 1, 0)

    def last_y(f):
        return pltpu.roll(f, 1, 0)

    def next_z(f):
        return jnp.where(last_lane, 0.0, pltpu.roll(f, lanes - 1, 1))

    def last_z(f):
        return jnp.where(first_lane, 0.0, pltpu.roll(f, 1, 1))

    for turn, (first, first_e, end_h, end_e) in enumerate(ranges):
        last = turn == margin - 1
        if product:
            both = ahead_z(first, end_h)
        held_y = held_z = None
        for i in range(first, end_e):
            ex, ey, ez = ext[0, i], ext[1, i], ext[2, i]
            hx, hy, hz = ext[3, i], ext[4, i], ext[5, i]
            if i < end_h:
                ey_x, ez_x = ext[1, i + 1], ext[2, i + 1]
                if turn == 0:
                    hx, hy, hz = hx * (1 / COURANT), hy * (1 / COURANT), hz * (1 / COURANT)
                if product:
                    ahead_x, ahead_y = (both[n * high : (n + 1) * high] for n in (i - first, i - first + end_h - first))
                else:
                    ahead_x, ahead_y = next_z(ex) - ex, next_z(ey) - ey
                hx = hx - ((next_y(ez) - ez) - ahead_y)
                hy = hy - (ahead_x - (ez_x - ez))
                hz = hz - ((ey_x - ey) - (next_y(ex) - ex))

                def clear(h):
                    h = jnp.concatenate([h[:rows], h[rows:] * before_rows], 0)
                    return h * before_x if i < margin else h

                hx, hy, hz = clear(hx), clear(hy), clear(hz)
                ext[3, i], ext[4, i], ext[5, i] = hx, hy, hz
            if i >= first_e:
                if held_y is None:
                    held_y, held_z = ext[4, i - 1], ext[5, i - 1]
                c = ext[6, i]
                ex = ex + c * ((hz - last_y(hz)) - (hy - last_z(hy)))
                ey = ey + c * ((hx - last_z(hx)) - (hz - held_z))
                ez = ez + c * ((hy - held_y) - (hx - last_y(hx)))
                if not last:
                    ext[0, i], ext[1, i], ext[2, i] = ex, ey, ez
                if margin <= i < margin + width:
                    x = i - margin
                    own_e = (ex[:rows], ey[:rows], ez[:rows])
                    total = sum(forward[turn, a, x].astype(jnp.float32) * own_e[a] for a in range(3))
                    if turn > 0:
                        total = total + masked[x]
                    if last:
                        total = total * mask[x].astype(jnp.float32)
                        for a in range(3):
                            final[a, x] = own_e[a]
                    masked[x] = total
            held_y, held_z = hy, hz


def inner_ranges(margin, width, core):
    top = width + 2 * margin - 1
    if core == 1:
        return [(t, t + 1, top - margin - t, top - margin - t) for t in range(margin)]
    return [(margin + t, margin + t + 1, top - t, top - t) for t in range(margin)]


def outer_ranges(margin, width, core):
    top = width + 2 * margin - 1
    if core == 1:
        return [(top - margin - t, top - margin - t, top - t, top - t) for t in range(margin)]
    return [(t, t + 1, margin + t, margin + t + 1) for t in range(margin)]


def early_steps(margin, count_y, ext_in, forward, mask, inner, ext, masked, final):
    del ext_in
    width, lanes = mask.shape[0], mask.shape[2]
    rows = mask.shape[1]
    _, at_y, core, _ = position()
    valid = valid_rows(low_half(lanes), at_y, count_y)
    in_at = (1 - core) * (width + margin)
    for k in range(7):
        for j in range(margin):
            tile = inner[k, j]
            ext[k, in_at + j, rows:] = jnp.where(valid, COURANT * COURANT / tile, 0.0) if k == 6 else tile
    for c in range(2):
        @pl.when(core == c)
        def _():
            steps(margin, inner_ranges(margin, width, c), True, ext, forward, mask, masked, final)


def late_steps(margin, reach, rounds, ext_in, masked_in, final_in, forward, mask, weights, ext, masked, final, send):
    del ext_in, masked_in, final_in
    _, _, core, _ = position()
    for c in range(2):
        @pl.when(core == c)
        def _():
            steps(margin, outer_ranges(margin, mask.shape[0], c), False, ext, forward, mask, masked, final)
    band_hop(reach, rounds, None, 1, True, weights, masked, send)


def band_sum(reach, hop, sign, alone, weights, own, other, where, sums):
    width, _, lanes = own.shape
    _, _, core, _ = position()
    middle = weights.shape[0] // 2
    for j in range(width):
        for same in (True,) if alone else (True, False):
            plane = (own if same else other)[j, where]
            for x in range(width):
                distances = [j - x - 2 * hop * s * width + (0 if same else t * width) for s in (1, -1) for t in (1, -1)]
                if min(abs(distance) for distance in distances) > reach:
                    continue
                distance = j - x - 2 * hop * width * sign + (0 if same else (1 - 2 * core) * width)
                weight = jnp.broadcast_to(weights[pl.ds(middle + distance, 1)], (SUB, lanes))
                sums[x] = sums[x] + weight * plane
    return sums


def arrived(count_x, via_1, via_0, x, where):
    at_x, _, core, _ = position()
    first, second = via_1[x, where], via_0[x, where]
    up = core == 1
    before = jnp.where(at_x >= 2, jnp.where(up, first, second), 0.0)
    after = jnp.where(at_x < count_x - 2, jnp.where(up, second, first), 0.0)
    return before, after


def band_hop(reach, hop, count_x, up, alone, weights, own, *refs):
    *refs, send = refs
    other, via = (own, refs) if alone else (refs[0], refs[1:])
    width, rows, lanes = own.shape
    _, _, core, _ = position()
    ahead = core == up
    for r in range(rows // SUB):
        where = slice(r * SUB, (r + 1) * SUB)
        if via:
            start = [jnp.where(ahead, *arrived(count_x, *via, x, where)) for x in range(width)]
        else:
            start = [jnp.zeros((SUB, lanes), jnp.float32)] * width
        sums = band_sum(reach, hop, jnp.where(ahead, 1, -1), alone, weights, own, other, where, start)
        for x in range(width):
            send[x, where] = sums[x]


def band_own(reach, weights, own, other, final, base, stored, sem):
    store = pltpu.make_async_copy(final, stored, sem)
    store.start()
    width, rows, lanes = own.shape
    for r in range(rows // SUB):
        where = slice(r * SUB, (r + 1) * SUB)
        sums = band_sum(reach, 0, 1, False, weights, own, other, where, [jnp.zeros((SUB, lanes), jnp.float32)] * width)
        for x in range(width):
            base[x, where] = sums[x]
    store.wait()


def band_end(count_x, base, via_1, via_0, out):
    for x in range(out.shape[0]):
        before, after = arrived(count_x, via_1, via_0, x, slice(None))
        out[x] = base[x] + before + after


def shards(routes, adjoint_fields, forward_e, permittivity, design_mask, band_offsets, filter_taps):
    width, rows, lanes = permittivity.shape
    margin = ITERS
    f32 = jnp.float32
    planes = sum(depths(margin))
    shape = jax.ShapeDtypeStruct
    vmem = pl.BlockSpec(memory_space=pltpu.VMEM)
    hbm = pl.BlockSpec(memory_space=pltpu.HBM)
    params = pltpu.CompilerParams(vmem_limit_bytes=24 * 1024 * 1024)
    block = shape((width, rows, lanes), f32)
    ext = shape((7, width + 2 * margin, rows + SUB, lanes), f32)
    strip = shape((planes, rows, lanes), f32)
    edge = shape((sum(side_tiles(width, margin)), SUB, lanes), f32)
    corner = shape((7, margin, SUB, lanes), f32)
    reach = width * routes.count_x // 4
    rounds = -(-reach // (2 * width))
    distances = shape((4 * (rounds + 1) * width, lanes), f32)

    def cost(microseconds):
        return pl.CostEstimate(flops=int(microseconds * 1e9), bytes_accessed=int(microseconds * 3.6e6), transcendentals=0)

    def move(value, pairs):
        return lax.ppermute(value, BOTH, pairs)

    def from_hbm(*values):
        return [pltpu.with_memory_space_constraint(value, pltpu.HBM) for value in values]

    cells, side_a0, side_b, side_a1 = pl.pallas_call(
        functools.partial(pack_y, margin),
        out_shape=(ext, edge, edge, edge),
        in_specs=[hbm] * 2,
        out_specs=(vmem,) * 4,
        scratch_shapes=[pltpu.SemaphoreType.DMA((7,))],
        compiler_params=params,
        name="pack_y",
    )(*from_hbm(adjoint_fields, permittivity))
    out_x, in_x = pl.pallas_call(
        functools.partial(pack_x, margin),
        out_shape=(strip, strip),
        in_specs=[vmem],
        out_specs=(vmem,) * 2,
        compiler_params=params,
        name="pack_x",
    )(cells)
    side_a0 = move(side_a0, routes.side_a[0])
    side_b = move(side_b, routes.side_b)
    side_a1 = move(side_a1, routes.side_a[1])
    in_x = move(in_x, routes.core)
    out_x = move(out_x, routes.out_x)
    cells, forward_e, design_mask, weights = pl.pallas_call(
        load_rest,
        out_shape=(ext, pltpu.VMEM(forward_e.shape, forward_e.dtype), pltpu.VMEM(design_mask.shape, design_mask.dtype), distances),
        in_specs=[vmem] + [hbm] * 4,
        out_specs=(vmem,) * 4,
        input_output_aliases={0: 0},
        scratch_shapes=[
            (pltpu.SMEM(band_offsets.shape, band_offsets.dtype), pltpu.SMEM(filter_taps.shape, filter_taps.dtype)),
            pltpu.SemaphoreType.DMA((4,)),
        ],
        compiler_params=params,
        cost_estimate=cost(JOIN_X_US),
        name="load_rest",
    )(cells, *from_hbm(forward_e, design_mask, band_offsets, filter_taps))
    cells, outer = pl.pallas_call(
        functools.partial(join_y, margin, routes.count_y),
        out_shape=(ext, corner),
        in_specs=[vmem] * 4,
        out_specs=(vmem,) * 2,
        input_output_aliases={0: 0},
        compiler_params=params,
        cost_estimate=cost(JOIN_Y_US),
        name="join_y",
    )(cells, side_a0, side_b, side_a1)
    outer = move(outer, routes.out_x)
    cells, inner = pl.pallas_call(
        functools.partial(join_inner, margin, routes.count_y),
        out_shape=(ext, corner),
        in_specs=[vmem],
        out_specs=(vmem,) * 2,
        input_output_aliases={0: 0},
        compiler_params=params,
        cost_estimate=cost(JOIN_X_US),
        name="join_inner",
    )(cells)
    inner = move(inner, routes.core)
    cells = pl.pallas_call(
        functools.partial(join_core, margin),
        out_shape=ext,
        in_specs=[vmem] * 2,
        out_specs=vmem,
        input_output_aliases={0: 0},
        compiler_params=params,
        cost_estimate=cost(JOIN_X_US),
        name="join_core",
    )(cells, in_x)
    fields = pltpu.VMEM((3, width, rows, lanes), f32)
    cells, masked, final = pl.pallas_call(
        functools.partial(early_steps, margin, routes.count_y),
        out_shape=(ext, block, fields),
        in_specs=[vmem] * 4,
        out_specs=(vmem,) * 3,
        input_output_aliases={0: 0},
        compiler_params=params,
        cost_estimate=cost(JOIN_X_US),
        name="early_steps",
    )(cells, forward_e, design_mask, inner)
    cells = pl.pallas_call(
        functools.partial(join_outer, margin, routes.count_x),
        out_shape=ext,
        in_specs=[vmem] * 2,
        out_specs=vmem,
        input_output_aliases={0: 0},
        compiler_params=params,
        cost_estimate=cost(JOIN_X_US),
        name="join_outer",
    )(cells, out_x)
    cells = pl.pallas_call(
        functools.partial(join_corner, margin, routes.count_x, routes.count_y),
        out_shape=ext,
        in_specs=[vmem] * 2,
        out_specs=vmem,
        input_output_aliases={0: 0},
        compiler_params=params,
        cost_estimate=cost(JOIN_X_US),
        name="join_corner",
    )(cells, outer)
    _, masked, final, send_1 = pl.pallas_call(
        functools.partial(late_steps, margin, reach, rounds),
        out_shape=(ext, block, fields, block),
        in_specs=[vmem] * 6,
        out_specs=(vmem,) * 4,
        input_output_aliases={0: 0, 1: 1, 2: 2},
        compiler_params=params,
        cost_estimate=cost(JOIN_X_US),
        name="late_steps",
    )(cells, masked, final, forward_e, design_mask, weights)

    other = move(masked, routes.core)
    via = []

    def hop_kernel(hop, up, alone):
        operands = [weights, masked] + ([] if alone else [other]) + via
        return pl.pallas_call(
            functools.partial(band_hop, reach, hop, routes.count_x, up, alone),
            out_shape=block,
            in_specs=[vmem] * len(operands),
            out_specs=vmem,
            compiler_params=params,
            name="band_hop",
        )(*operands)

    for hop in range(rounds, 0, -1):
        if hop < rounds:
            send_1 = hop_kernel(hop, 1, False)
        send_0 = hop_kernel(hop, 0, False)
        via = [move(send_1, routes.ring_1), move(send_0, routes.ring_0)]
    base, final = pl.pallas_call(
        functools.partial(band_own, reach),
        out_shape=(block, shape(final.shape, f32)),
        in_specs=[vmem] * 4,
        out_specs=(vmem, hbm),
        scratch_shapes=[pltpu.SemaphoreType.DMA],
        compiler_params=params,
        cost_estimate=cost(BAND_OWN_US),
        name="band_own",
    )(weights, masked, other, final)
    filtered = pl.pallas_call(
        functools.partial(band_end, routes.count_x),
        out_shape=block,
        in_specs=[vmem] * 3,
        out_specs=vmem,
        compiler_params=params,
        name="band_end",
    )(base, *via)
    return filtered, final


def solution(mesh):
    routes = Routes(mesh.shape["gx"], mesh.shape["gy"])
    return jax.shard_map(
        functools.partial(shards, routes),
        mesh=mesh,
        in_specs=(
            P(None, "gx", "gy", None),
            P(None, None, "gx", "gy", None),
            P("gx", "gy", None),
            P("gx", "gy", None),
            P(),
            P(),
        ),
        out_specs=(P("gx", "gy", None), P(None, "gx", "gy", None)),
        check_vma=False,
    )
```

```python
import functools
import jax
import jax.numpy as jnp
from jax import lax
from jax.experimental import pallas as pl
from jax.experimental.pallas import tpu as pltpu
from jax.sharding import PartitionSpec as P

ITERS = 4
COURANT = 0.5
BOTH = ("gx", "gy")
SUB = 8
JOIN_Y_US = 50
JOIN_X_US = 0.05
BAND_OWN_US = 2


def swaps(count_x, count_y, partner, idle):
    pairs = []
    for x in range(count_x):
        for y in range(count_y):
            to = partner(x, y)
            if to is None:
                to = idle(x, y)
            pairs.append((x * count_y + y, to[0] * count_y + to[1]))
    assert sorted(b for _, b in pairs) == sorted(a for a, _ in pairs)
    return pairs


class Routes:
    def __init__(self, count_x, count_y):
        self.count_x, self.count_y = count_x, count_y
        round_y = [y ^ (y >> 1) for y in range(count_y)]
        if sorted(round_y) != list(range(count_y)):
            round_y = list(range(count_y))

        def outward_x(x):
            to = x + 1 if x % 2 else x - 1
            return to if 0 <= to < count_x else None

        def side_b(y):
            to = y + 1 if y % 2 else y - 1
            return to if 0 <= to < count_y else None

        def around(x, y):
            return (x, round_y[(round_y.index(y) + 1) % count_y])

        def out_partner(x, y):
            return None if outward_x(x) is None else (outward_x(x), y)

        def b_partner(x, y):
            return None if side_b(y) is None else (x, side_b(y))

        def ring(x, y, up):
            to = x + 2 if x % 2 == up else x - 2
            return (to, y) if 0 <= to < count_x else (x ^ 1, y)

        make = functools.partial(swaps, count_x, count_y)
        core = lambda x, y: (x ^ 1, y)
        self.core = make(core, None)
        self.out_x = make(out_partner, around)
        self.side_a = [make(lambda x, y: (x, y ^ 1) if y // 2 % 2 == n else None, core) for n in range(2)]
        self.side_b = make(b_partner, core)
        self.ring_1 = make(lambda x, y: ring(x, y, 1), None)
        self.ring_0 = make(lambda x, y: ring(x, y, 0), None)


def depths(margin):
    return (margin, margin, margin, margin - 1, margin, margin, margin - 1)


def edge_tile(low, first, second, upper):
    up = upper == 1
    first = jnp.where(up, pltpu.roll(first, SUB // 2, 0), first)
    second = jnp.where(up, second, pltpu.roll(second, SUB // 2, 0))
    return jnp.where(low, first, second)


def tail_tile(low, odd, from_a, from_b, upper):
    after = jnp.where(odd == 0, from_a, from_b)
    before = jnp.where(odd == 0, from_b, from_a)
    if upper:
        after = pltpu.roll(after, SUB // 2, 0)
    else:
        before = pltpu.roll(before, SUB // 2, 0)
    return jnp.where(low, after, before)


SHORT = (4, 6)
LONG = (0, 1, 2, 3, 5)


def short_places(width, depth):
    for n, (k, x) in enumerate((k, x) for k in SHORT for x in range(width)):
        yield k, x, n * depth // SUB, n * depth % SUB


def side_tiles(width, margin):
    assert margin * 2 == SUB
    return len(LONG) * width // 2, -(-len(SHORT) * width * (margin - 1) // SUB)


def low_half(lanes):
    return lax.broadcasted_iota(jnp.int32, (SUB, lanes), 0) < SUB // 2


def position():
    at_x, at_y = lax.axis_index("gx"), lax.axis_index("gy")
    return at_x, at_y, lax.rem(at_x, 2), lax.rem(at_y, 2)


def pack_y(margin, fields, perm, ext, side_a0, side_b, side_a1, sems):
    width, rows, lanes = perm.shape
    _, _, _, odd = position()
    low = low_half(lanes)
    own = (pl.ds(margin, width), pl.ds(0, rows))
    loads = [pltpu.make_async_copy(fields.at[k] if k < 6 else perm, ext.at[(k, *own)], sems.at[k]) for k in range(7)]
    for load in loads:
        load.start()

    def rows_of(k, x, upper):
        return ext[k, margin + x, pl.ds(pl.multiple_of(upper * (rows - SUB), SUB), SUB)]

    for k in range(7):
        loads[k].wait()
        if k in LONG:
            for j in range(width // 2):
                for upper, to in ((1 - odd, (side_a0, side_a1)), (odd, (side_b,))):
                    tile = edge_tile(low, rows_of(k, j, upper), rows_of(k, j + width // 2, upper), upper)
                    for ref in to:
                        ref[LONG.index(k) * (width // 2) + j] = tile
    long_tiles, _ = side_tiles(width, margin)
    depth = margin - 1
    sub = lax.broadcasted_iota(jnp.int32, (SUB, lanes), 0)
    for upper, to in ((1 - odd, (side_a0, side_a1)), (odd, (side_b,))):
        tiles = {}
        for k, x, t, at in short_places(width, depth):
            rows_kx = rows_of(k, x, upper)
            rows_kx = jnp.where(upper == 1, pltpu.roll(rows_kx, depth, 0), rows_kx)
            rows_kx = pltpu.roll(rows_kx, at, 0) if at else rows_kx
            tiles[t] = jnp.where(sub >= at, rows_kx, tiles[t]) if t in tiles else rows_kx
            if at + depth > SUB:
                tiles[t + 1] = rows_kx
        for t, tile in tiles.items():
            for ref in to:
                ref[long_tiles + t] = tile


def pack_x(margin, ext, out_x, in_x):
    width, rows = ext.shape[1] - 2 * margin, ext.shape[2] - SUB
    _, _, core, _ = position()
    at = 0
    for k, depth in enumerate(depths(margin)):
        for j in range(depth):
            out_x[at + j] = ext[k, margin + core * (width - depth) + j, 0:rows]
            in_x[at + j] = ext[k, margin + (1 - core) * (width - depth) + j, 0:rows]
        at += depth


def valid_rows(low, at_y, count_y):
    return jnp.where(low, jnp.where(at_y < count_y - 1, 1, 0), jnp.where(at_y > 0, 1, 0)) > 0


def has_outward(at_x, core, count_x):
    return jnp.where(core == 0, at_x > 0, at_x < count_x - 1)


def join_y(margin, count_y, ext_in, side_a0, side_b, side_a1, ext, outer):
    del ext_in
    width, rows, lanes = ext.shape[1] - 2 * margin, ext.shape[2] - SUB, ext.shape[3]
    _, at_y, core, odd = position()
    low = low_half(lanes)
    has_after, has_before = at_y < count_y - 1, at_y > 0
    valid = valid_rows(low, at_y, count_y)
    in_first = lax.rem(at_y // 2, 2) == 0
    long_tiles, short_tiles = side_tiles(width, margin)
    depth = margin - 1
    sub = lax.broadcasted_iota(jnp.int32, (SUB, lanes), 0)

    def from_sides(t):
        side_a = jnp.where(in_first, side_a0[t], side_a1[t])
        return side_a, side_b[t]

    after, before = [], []
    for t in range(short_tiles):
        from_a, from_b = from_sides(long_tiles + t)
        after.append(jnp.where(odd == 0, from_a, from_b))
        before.append(jnp.where(odd == 0, from_b, from_a))

    def short_rows(tiles, t, at, to):
        tile = tiles[t]
        if at + depth > SUB:
            tile = jnp.where(sub >= at, tile, tiles[t + 1])
        return pltpu.roll(tile, (to - at) % SUB, 0) if (to - at) % SUB else tile

    for k, x, t, at in short_places(width, depth):
        blank = 1.0 if k == 6 else 0.0
        tile = jnp.where((sub < depth) & jnp.broadcast_to(has_after, (SUB, lanes)), short_rows(after, t, at, 0), blank)
        upper_rows = (sub >= SUB - depth) & jnp.broadcast_to(has_before, (SUB, lanes))
        ext[k, margin + x, rows:] = jnp.where(upper_rows, short_rows(before, t, at, SUB - depth), tile)
    for k in range(7):
        for x in range(width if k in LONG else 0):
            j, upper = x % (width // 2), x // (width // 2)
            tile = tail_tile(low, odd, *from_sides(LONG.index(k) * (width // 2) + j), upper)
            ext[k, margin + x, rows:] = jnp.where(valid, tile, 0.0)
    at = 0
    for k, depth in enumerate(depths(margin)):
        for j in range(depth):
            outer[at + j] = ext[k, margin + core * (width - depth) + j, rows:]
        at += depth


def join_inner(margin, count_y, ext_in, ext, inner):
    del ext_in
    width, rows, lanes = ext.shape[1] - 2 * margin, ext.shape[2] - SUB, ext.shape[3]
    _, at_y, core, _ = position()
    valid = valid_rows(low_half(lanes), at_y, count_y)
    at = 0
    for k, depth in enumerate(depths(margin)):
        for j in range(depth):
            inner[at + j] = ext[k, margin + (1 - core) * (width - depth) + j, rows:]
        at += depth
    scale = COURANT * COURANT
    for x in range(margin, margin + width):
        ext[6, x, 0:rows] = scale / ext[6, x, 0:rows]
        ext[6, x, rows:] = jnp.where(valid, scale / ext[6, x, rows:], 0.0)


def load_rest(ext_in, forward, mask, offsets, taps, ext, forward_out, mask_out, weights, table, sems):
    del ext_in, ext
    lists = [pltpu.make_async_copy(offsets, table[0], sems.at[0]), pltpu.make_async_copy(taps, table[1], sems.at[1])]
    loads = [pltpu.make_async_copy(forward, forward_out, sems.at[2]), pltpu.make_async_copy(mask, mask_out, sems.at[3])]
    for load in lists + loads:
        load.start()
    for load in lists:
        load.wait()
    distance = lax.broadcasted_iota(jnp.int32, weights.shape, 0) - weights.shape[0] // 2
    total = jnp.zeros(weights.shape, jnp.float32)
    for b in range(offsets.shape[0]):
        total = total + jnp.where(distance == table[0][b], table[1][b], 0.0)
    weights[...] = total
    for load in loads:
        load.wait()


def join_core(margin, ext_in, in_x, ext):
    del ext_in
    width, rows = ext.shape[1] - 2 * margin, ext.shape[2] - SUB
    _, _, core, _ = position()
    in_at = (1 - core) * (width + margin)
    at = 0
    for k, depth in enumerate(depths(margin)):
        for j in range(depth):
            plane = in_x[at + j]
            plane = COURANT * COURANT / plane if k == 6 else plane
            ext[k, in_at + core * (margin - depth) + j, 0:rows] = plane
        at += depth


def join_outer(margin, count_x, ext_in, out_x, ext):
    del ext_in
    width, rows = ext.shape[1] - 2 * margin, ext.shape[2] - SUB
    at_x, _, core, _ = position()
    has_out = has_outward(at_x, core, count_x)
    out_at = core * (width + margin)
    at = 0
    for k, depth in enumerate(depths(margin)):
        for j in range(depth):
            plane = out_x[at + j]
            plane = COURANT * COURANT / plane if k == 6 else plane
            ext[k, out_at + (1 - core) * (margin - depth) + j, 0:rows] = jnp.where(has_out, plane, 0.0)
        at += depth


def join_corner(margin, count_x, count_y, ext_in, outer, ext):
    del ext_in
    width, rows, lanes = ext.shape[1] - 2 * margin, ext.shape[2] - SUB, ext.shape[3]
    at_x, at_y, core, _ = position()
    has_out = has_outward(at_x, core, count_x)
    valid = valid_rows(low_half(lanes), at_y, count_y) & jnp.broadcast_to(has_out, (SUB, lanes))
    out_at = core * (width + margin)
    at = 0
    for k, depth in enumerate(depths(margin)):
        for j in range(depth):
            tile = outer[at + j]
            tile = jnp.where(valid, COURANT * COURANT / tile, 0.0) if k == 6 else jnp.where(has_out, tile, 0.0)
            ext[k, out_at + (1 - core) * (margin - depth) + j, rows:] = tile
        at += depth


def steps(margin, ranges, product, ext, forward, mask, masked, final):
    width, rows, lanes = mask.shape
    high = rows + SUB
    at_x, at_y, _, _ = position()
    low = low_half(lanes)
    lane = lax.broadcasted_iota(jnp.int32, (high, lanes), 1)
    first_lane, last_lane = lane == 0, lane == lanes - 1
    before_rows = jnp.where(low | jnp.broadcast_to(at_y > 0, (SUB, lanes)), 1.0, 0.0)
    before_x = jnp.where(at_x > 0, 1.0, 0.0)

    gap = lax.broadcasted_iota(jnp.int32, (lanes, lanes), 0) - lax.broadcasted_iota(jnp.int32, (lanes, lanes), 1)
    ahead = jnp.where(gap == 1, 1.0, 0.0) - jnp.where(gap == 0, 1.0, 0.0)
    ahead = jnp.concatenate([ahead, ahead], 0).astype(jnp.bfloat16)

    def ahead_z(first, end):
        f = ext[0:2, first:end].reshape(2 * (end - first) * high, lanes)
        main = f.astype(jnp.bfloat16)
        rest = (f - main.astype(jnp.float32)).astype(jnp.bfloat16)
        return jnp.dot(jnp.concatenate([main, rest], 1), ahead, preferred_element_type=jnp.float32)

    def next_y(f):
        return pltpu.roll(f, high - 1, 0)

    def last_y(f):
        return pltpu.roll(f, 1, 0)

    def next_z(f):
        return jnp.where(last_lane, 0.0, pltpu.roll(f, lanes - 1, 1))

    def last_z(f):
        return jnp.where(first_lane, 0.0, pltpu.roll(f, 1, 1))

    for turn, (first, first_e, end_h, end_e) in enumerate(ranges):
        last = turn == margin - 1
        if product:
            both = ahead_z(first, end_h)
        held_y = held_z = None
        for i in range(first, end_e):
            ex, ey, ez = ext[0, i], ext[1, i], ext[2, i]
            hx, hy, hz = ext[3, i], ext[4, i], ext[5, i]
            if i < end_h:
                ey_x, ez_x = ext[1, i + 1], ext[2, i + 1]
                if turn == 0:
                    hx, hy, hz = hx * (1 / COURANT), hy * (1 / COURANT), hz * (1 / COURANT)
                if product:
                    ahead_x, ahead_y = (both[n * high : (n + 1) * high] for n in (i - first, i - first + end_h - first))
                else:
                    ahead_x, ahead_y = next_z(ex) - ex, next_z(ey) - ey
                hx = hx - ((next_y(ez) - ez) - ahead_y)
                hy = hy - (ahead_x - (ez_x - ez))
                hz = hz - ((ey_x - ey) - (next_y(ex) - ex))

                def clear(h):
                    h = jnp.concatenate([h[:rows], h[rows:] * before_rows], 0)
                    return h * before_x if i < margin else h

                hx, hy, hz = clear(hx), clear(hy), clear(hz)
                ext[3, i], ext[4, i], ext[5, i] = hx, hy, hz
            if i >= first_e:
                if held_y is None:
                    held_y, held_z = ext[4, i - 1], ext[5, i - 1]
                c = ext[6, i]
                ex = ex + c * ((hz - last_y(hz)) - (hy - last_z(hy)))
                ey = ey + c * ((hx - last_z(hx)) - (hz - held_z))
                ez = ez + c * ((hy - held_y) - (hx - last_y(hx)))
                if not last:
                    ext[0, i], ext[1, i], ext[2, i] = ex, ey, ez
                if margin <= i < margin + width:
                    x = i - margin
                    own_e = (ex[:rows], ey[:rows], ez[:rows])
                    total = sum(forward[turn, a, x].astype(jnp.float32) * own_e[a] for a in range(3))
                    if turn > 0:
                        total = total + masked[x]
                    if last:
                        total = total * mask[x].astype(jnp.float32)
                        for a in range(3):
                            final[a, x] = own_e[a]
                    masked[x] = total
            held_y, held_z = hy, hz


def inner_ranges(margin, width, core):
    top = width + 2 * margin - 1
    if core == 1:
        return [(t, t + 1, top - margin - t, top - margin - t) for t in range(margin)]
    return [(margin + t, margin + t + 1, top - t, top - t) for t in range(margin)]


def outer_ranges(margin, width, core):
    top = width + 2 * margin - 1
    if core == 1:
        return [(top - margin - t, top - margin - t, top - t, top - t) for t in range(margin)]
    return [(t, t + 1, margin + t, margin + t + 1) for t in range(margin)]


def early_steps(margin, count_y, ext_in, forward, mask, inner, ext, masked, final):
    del ext_in
    width, lanes = mask.shape[0], mask.shape[2]
    rows = mask.shape[1]
    _, at_y, core, _ = position()
    valid = valid_rows(low_half(lanes), at_y, count_y)
    in_at = (1 - core) * (width + margin)
    at = 0
    for k, depth in enumerate(depths(margin)):
        for j in range(depth):
            tile = inner[at + j]
            place = in_at + core * (margin - depth) + j
            ext[k, place, rows:] = jnp.where(valid, COURANT * COURANT / tile, 0.0) if k == 6 else tile
        at += depth
    for c in range(2):
        @pl.when(core == c)
        def _():
            steps(margin, inner_ranges(margin, width, c), True, ext, forward, mask, masked, final)


def late_steps(margin, reach, rounds, ext_in, masked_in, final_in, forward, mask, weights, ext, masked, final, send):
    del ext_in, masked_in, final_in
    _, _, core, _ = position()
    for c in range(2):
        @pl.when(core == c)
        def _():
            steps(margin, outer_ranges(margin, mask.shape[0], c), False, ext, forward, mask, masked, final)
    band_hop(reach, rounds, None, 1, True, weights, masked, send)


def band_sum(reach, hop, sign, alone, weights, own, other, where, sums):
    width, _, lanes = own.shape
    _, _, core, _ = position()
    middle = weights.shape[0] // 2
    for j in range(width):
        for same in (True,) if alone else (True, False):
            plane = (own if same else other)[j, where]
            for x in range(width):
                distances = [j - x - 2 * hop * s * width + (0 if same else t * width) for s in (1, -1) for t in (1, -1)]
                if min(abs(distance) for distance in distances) > reach:
                    continue
                distance = j - x - 2 * hop * width * sign + (0 if same else (1 - 2 * core) * width)
                weight = jnp.broadcast_to(weights[pl.ds(middle + distance, 1)], (SUB, lanes))
                sums[x] = sums[x] + weight * plane
    return sums


def arrived(count_x, via_1, via_0, x, where):
    at_x, _, core, _ = position()
    first, second = via_1[x, where], via_0[x, where]
    up = core == 1
    before = jnp.where(at_x >= 2, jnp.where(up, first, second), 0.0)
    after = jnp.where(at_x < count_x - 2, jnp.where(up, second, first), 0.0)
    return before, after


def band_hop(reach, hop, count_x, up, alone, weights, own, *refs):
    *refs, send = refs
    other, via = (own, refs) if alone else (refs[0], refs[1:])
    width, rows, lanes = own.shape
    _, _, core, _ = position()
    ahead = core == up
    for r in range(rows // SUB):
        where = slice(r * SUB, (r + 1) * SUB)
        if via:
            start = [jnp.where(ahead, *arrived(count_x, *via, x, where)) for x in range(width)]
        else:
            start = [jnp.zeros((SUB, lanes), jnp.float32)] * width
        sums = band_sum(reach, hop, jnp.where(ahead, 1, -1), alone, weights, own, other, where, start)
        for x in range(width):
            send[x, where] = sums[x]


def band_own(reach, weights, own, other, final, base, stored, sem):
    store = pltpu.make_async_copy(final, stored, sem)
    store.start()
    width, rows, lanes = own.shape
    for r in range(rows // SUB):
        where = slice(r * SUB, (r + 1) * SUB)
        sums = band_sum(reach, 0, 1, False, weights, own, other, where, [jnp.zeros((SUB, lanes), jnp.float32)] * width)
        for x in range(width):
            base[x, where] = sums[x]
    store.wait()


def band_end(count_x, base, via_1, via_0, out):
    for x in range(out.shape[0]):
        before, after = arrived(count_x, via_1, via_0, x, slice(None))
        out[x] = base[x] + before + after


def shards(routes, adjoint_fields, forward_e, permittivity, design_mask, band_offsets, filter_taps):
    width, rows, lanes = permittivity.shape
    margin = ITERS
    f32 = jnp.float32
    planes = sum(depths(margin))
    shape = jax.ShapeDtypeStruct
    vmem = pl.BlockSpec(memory_space=pltpu.VMEM)
    hbm = pl.BlockSpec(memory_space=pltpu.HBM)
    params = pltpu.CompilerParams(vmem_limit_bytes=24 * 1024 * 1024)
    block = shape((width, rows, lanes), f32)
    ext = shape((7, width + 2 * margin, rows + SUB, lanes), f32)
    strip = shape((planes, rows, lanes), f32)
    edge = shape((sum(side_tiles(width, margin)), SUB, lanes), f32)
    corner = shape((planes, SUB, lanes), f32)
    reach = width * routes.count_x // 4
    rounds = -(-reach // (2 * width))
    distances = shape((4 * (rounds + 1) * width, lanes), f32)

    def cost(microseconds):
        return pl.CostEstimate(flops=int(microseconds * 1e9), bytes_accessed=int(microseconds * 3.6e6), transcendentals=0)

    def move(value, pairs):
        return lax.ppermute(value, BOTH, pairs)

    def from_hbm(*values):
        return [pltpu.with_memory_space_constraint(value, pltpu.HBM) for value in values]

    cells, side_a0, side_b, side_a1 = pl.pallas_call(
        functools.partial(pack_y, margin),
        out_shape=(ext, edge, edge, edge),
        in_specs=[hbm] * 2,
        out_specs=(vmem,) * 4,
        scratch_shapes=[pltpu.SemaphoreType.DMA((7,))],
        compiler_params=params,
        name="pack_y",
    )(*from_hbm(adjoint_fields, permittivity))
    out_x, in_x = pl.pallas_call(
        functools.partial(pack_x, margin),
        out_shape=(strip, strip),
        in_specs=[vmem],
        out_specs=(vmem,) * 2,
        compiler_params=params,
        name="pack_x",
    )(cells)
    side_a0 = move(side_a0, routes.side_a[0])
    side_b = move(side_b, routes.side_b)
    side_a1 = move(side_a1, routes.side_a[1])
    in_x = move(in_x, routes.core)
    out_x = move(out_x, routes.out_x)
    cells, forward_e, design_mask, weights = pl.pallas_call(
        load_rest,
        out_shape=(ext, pltpu.VMEM(forward_e.shape, forward_e.dtype), pltpu.VMEM(design_mask.shape, design_mask.dtype), distances),
        in_specs=[vmem] + [hbm] * 4,
        out_specs=(vmem,) * 4,
        input_output_aliases={0: 0},
        scratch_shapes=[
            (pltpu.SMEM(band_offsets.shape, band_offsets.dtype), pltpu.SMEM(filter_taps.shape, filter_taps.dtype)),
            pltpu.SemaphoreType.DMA((4,)),
        ],
        compiler_params=params,
        cost_estimate=cost(JOIN_X_US),
        name="load_rest",
    )(cells, *from_hbm(forward_e, design_mask, band_offsets, filter_taps))
    cells, outer = pl.pallas_call(
        functools.partial(join_y, margin, routes.count_y),
        out_shape=(ext, corner),
        in_specs=[vmem] * 4,
        out_specs=(vmem,) * 2,
        input_output_aliases={0: 0},
        compiler_params=params,
        cost_estimate=cost(JOIN_Y_US),
        name="join_y",
    )(cells, side_a0, side_b, side_a1)
    outer = move(outer, routes.out_x)
    cells, inner = pl.pallas_call(
        functools.partial(join_inner, margin, routes.count_y),
        out_shape=(ext, corner),
        in_specs=[vmem],
        out_specs=(vmem,) * 2,
        input_output_aliases={0: 0},
        compiler_params=params,
        cost_estimate=cost(JOIN_X_US),
        name="join_inner",
    )(cells)
    inner = move(inner, routes.core)
    cells = pl.pallas_call(
        functools.partial(join_core, margin),
        out_shape=ext,
        in_specs=[vmem] * 2,
        out_specs=vmem,
        input_output_aliases={0: 0},
        compiler_params=params,
        cost_estimate=cost(JOIN_X_US),
        name="join_core",
    )(cells, in_x)
    fields = pltpu.VMEM((3, width, rows, lanes), f32)
    cells, masked, final = pl.pallas_call(
        functools.partial(early_steps, margin, routes.count_y),
        out_shape=(ext, block, fields),
        in_specs=[vmem] * 4,
        out_specs=(vmem,) * 3,
        input_output_aliases={0: 0},
        compiler_params=params,
        cost_estimate=cost(JOIN_X_US),
        name="early_steps",
    )(cells, forward_e, design_mask, inner)
    cells = pl.pallas_call(
        functools.partial(join_outer, margin, routes.count_x),
        out_shape=ext,
        in_specs=[vmem] * 2,
        out_specs=vmem,
        input_output_aliases={0: 0},
        compiler_params=params,
        cost_estimate=cost(JOIN_X_US),
        name="join_outer",
    )(cells, out_x)
    cells = pl.pallas_call(
        functools.partial(join_corner, margin, routes.count_x, routes.count_y),
        out_shape=ext,
        in_specs=[vmem] * 2,
        out_specs=vmem,
        input_output_aliases={0: 0},
        compiler_params=params,
        cost_estimate=cost(JOIN_X_US),
        name="join_corner",
    )(cells, outer)
    _, masked, final, send_1 = pl.pallas_call(
        functools.partial(late_steps, margin, reach, rounds),
        out_shape=(ext, block, fields, block),
        in_specs=[vmem] * 6,
        out_specs=(vmem,) * 4,
        input_output_aliases={0: 0, 1: 1, 2: 2},
        compiler_params=params,
        cost_estimate=cost(JOIN_X_US),
        name="late_steps",
    )(cells, masked, final, forward_e, design_mask, weights)

    other = move(masked, routes.core)
    via = []

    def hop_kernel(hop, up, alone):
        operands = [weights, masked] + ([] if alone else [other]) + via
        return pl.pallas_call(
            functools.partial(band_hop, reach, hop, routes.count_x, up, alone),
            out_shape=block,
            in_specs=[vmem] * len(operands),
            out_specs=vmem,
            compiler_params=params,
            name="band_hop",
        )(*operands)

    for hop in range(rounds, 0, -1):
        if hop < rounds:
            send_1 = hop_kernel(hop, 1, False)
        send_0 = hop_kernel(hop, 0, False)
        via = [move(send_1, routes.ring_1), move(send_0, routes.ring_0)]
    base, final = pl.pallas_call(
        functools.partial(band_own, reach),
        out_shape=(block, shape(final.shape, f32)),
        in_specs=[vmem] * 4,
        out_specs=(vmem, hbm),
        scratch_shapes=[pltpu.SemaphoreType.DMA],
        compiler_params=params,
        cost_estimate=cost(BAND_OWN_US),
        name="band_own",
    )(weights, masked, other, final)
    filtered = pl.pallas_call(
        functools.partial(band_end, routes.count_x),
        out_shape=block,
        in_specs=[vmem] * 3,
        out_specs=vmem,
        compiler_params=params,
        name="band_end",
    )(base, *via)
    return filtered, final


def solution(mesh):
    routes = Routes(mesh.shape["gx"], mesh.shape["gy"])
    return jax.shard_map(
        functools.partial(shards, routes),
        mesh=mesh,
        in_specs=(
            P(None, "gx", "gy", None),
            P(None, None, "gx", "gy", None),
            P("gx", "gy", None),
            P("gx", "gy", None),
            P(),
            P(),
        ),
        out_specs=(P("gx", "gy", None), P(None, "gx", "gy", None)),
        check_vma=False,
    )
```

```python
import functools
import jax
import jax.numpy as jnp
from jax import lax
from jax.experimental import pallas as pl
from jax.experimental.pallas import tpu as pltpu
from jax.sharding import PartitionSpec as P

ITERS = 4
COURANT = 0.5
BOTH = ("gx", "gy")
SUB = 8
JOIN_Y_US = 50
JOIN_X_US = 0.05
BAND_OWN_US = 2


def swaps(count_x, count_y, partner, idle):
    pairs = []
    for x in range(count_x):
        for y in range(count_y):
            to = partner(x, y)
            if to is None:
                to = idle(x, y)
            pairs.append((x * count_y + y, to[0] * count_y + to[1]))
    assert sorted(b for _, b in pairs) == sorted(a for a, _ in pairs)
    return pairs


class Routes:
    def __init__(self, count_x, count_y):
        self.count_x, self.count_y = count_x, count_y
        round_y = [y ^ (y >> 1) for y in range(count_y)]
        if sorted(round_y) != list(range(count_y)):
            round_y = list(range(count_y))

        def outward_x(x):
            to = x + 1 if x % 2 else x - 1
            return to if 0 <= to < count_x else None

        def side_b(y):
            to = y + 1 if y % 2 else y - 1
            return to if 0 <= to < count_y else None

        def around(x, y):
            return (x, round_y[(round_y.index(y) + 1) % count_y])

        def out_partner(x, y):
            return None if outward_x(x) is None else (outward_x(x), y)

        def b_partner(x, y):
            return None if side_b(y) is None else (x, side_b(y))

        def ring(x, y, up):
            to = x + 2 if x % 2 == up else x - 2
            return (to, y) if 0 <= to < count_x else (x ^ 1, y)

        make = functools.partial(swaps, count_x, count_y)
        core = lambda x, y: (x ^ 1, y)
        self.core = make(core, None)
        self.out_x = make(out_partner, around)
        self.side_a = [make(lambda x, y: (x, y ^ 1) if y // 2 % 2 == n else None, core) for n in range(2)]
        self.side_b = make(b_partner, core)
        self.ring_1 = make(lambda x, y: ring(x, y, 1), None)
        self.ring_0 = make(lambda x, y: ring(x, y, 0), None)


def depths(margin):
    return (margin, margin, margin, margin - 1, margin, margin, margin - 1)


def edge_tile(low, first, second, upper):
    up = upper == 1
    first = jnp.where(up, pltpu.roll(first, SUB // 2, 0), first)
    second = jnp.where(up, second, pltpu.roll(second, SUB // 2, 0))
    return jnp.where(low, first, second)


def tail_tile(low, odd, from_a, from_b, upper):
    after = jnp.where(odd == 0, from_a, from_b)
    before = jnp.where(odd == 0, from_b, from_a)
    if upper:
        after = pltpu.roll(after, SUB // 2, 0)
    else:
        before = pltpu.roll(before, SUB // 2, 0)
    return jnp.where(low, after, before)


SHORT = (4, 6)
LONG = (0, 1, 2, 3, 5)


def short_places(width, depth):
    for n, (k, x) in enumerate((k, x) for k in SHORT for x in range(width)):
        yield k, x, n * depth // SUB, n * depth % SUB


def side_tiles(width, margin):
    assert margin * 2 == SUB
    return len(LONG) * width // 2, -(-len(SHORT) * width * (margin - 1) // SUB)


def low_half(lanes):
    return lax.broadcasted_iota(jnp.int32, (SUB, lanes), 0) < SUB // 2


def position():
    at_x, at_y = lax.axis_index("gx"), lax.axis_index("gy")
    return at_x, at_y, lax.rem(at_x, 2), lax.rem(at_y, 2)


def pack_y(margin, fields, perm, ext, side_a0, side_b, side_a1, sems):
    width, rows, lanes = perm.shape
    _, _, _, odd = position()
    low = low_half(lanes)
    own = (pl.ds(margin, width), pl.ds(0, rows))
    loads = [pltpu.make_async_copy(fields.at[k] if k < 6 else perm, ext.at[(k, *own)], sems.at[k]) for k in range(7)]
    for load in loads:
        load.start()

    def rows_of(k, x, upper):
        return ext[k, margin + x, pl.ds(pl.multiple_of(upper * (rows - SUB), SUB), SUB)]

    for k in range(7):
        loads[k].wait()
        if k in LONG:
            for j in range(width // 2):
                for upper, to in ((1 - odd, (side_a0, side_a1)), (odd, (side_b,))):
                    tile = edge_tile(low, rows_of(k, j, upper), rows_of(k, j + width // 2, upper), upper)
                    for ref in to:
                        ref[LONG.index(k) * (width // 2) + j] = tile
    long_tiles, _ = side_tiles(width, margin)
    depth = margin - 1
    sub = lax.broadcasted_iota(jnp.int32, (SUB, lanes), 0)
    for upper, to in ((1 - odd, (side_a0, side_a1)), (odd, (side_b,))):
        tiles = {}
        for k, x, t, at in short_places(width, depth):
            rows_kx = rows_of(k, x, upper)
            rows_kx = jnp.where(upper == 1, pltpu.roll(rows_kx, depth, 0), rows_kx)
            rows_kx = pltpu.roll(rows_kx, at, 0) if at else rows_kx
            tiles[t] = jnp.where(sub >= at, rows_kx, tiles[t]) if t in tiles else rows_kx
            if at + depth > SUB:
                tiles[t + 1] = rows_kx
        for t, tile in tiles.items():
            for ref in to:
                ref[long_tiles + t] = tile


def pack_x(margin, ext, out_x, in_x):
    width, rows = ext.shape[1] - 2 * margin, ext.shape[2] - SUB
    _, _, core, _ = position()
    at = 0
    for k, depth in enumerate(depths(margin)):
        for j in range(depth):
            out_x[at + j] = ext[k, margin + core * (width - depth) + j, 0:rows]
            in_x[at + j] = ext[k, margin + (1 - core) * (width - depth) + j, 0:rows]
        at += depth


def valid_rows(low, at_y, count_y):
    return jnp.where(low, jnp.where(at_y < count_y - 1, 1, 0), jnp.where(at_y > 0, 1, 0)) > 0


def has_outward(at_x, core, count_x):
    return jnp.where(core == 0, at_x > 0, at_x < count_x - 1)


def join_y(margin, count_y, ext_in, side_a0, side_b, side_a1, ext, outer):
    del ext_in
    width, rows, lanes = ext.shape[1] - 2 * margin, ext.shape[2] - SUB, ext.shape[3]
    _, at_y, core, odd = position()
    low = low_half(lanes)
    has_after, has_before = at_y < count_y - 1, at_y > 0
    valid = valid_rows(low, at_y, count_y)
    in_first = lax.rem(at_y // 2, 2) == 0
    long_tiles, short_tiles = side_tiles(width, margin)
    depth = margin - 1
    sub = lax.broadcasted_iota(jnp.int32, (SUB, lanes), 0)

    def from_sides(t):
        side_a = jnp.where(in_first, side_a0[t], side_a1[t])
        return side_a, side_b[t]

    after, before = [], []
    for t in range(short_tiles):
        from_a, from_b = from_sides(long_tiles + t)
        after.append(jnp.where(odd == 0, from_a, from_b))
        before.append(jnp.where(odd == 0, from_b, from_a))

    def short_rows(tiles, t, at, to):
        tile = tiles[t]
        if at + depth > SUB:
            tile = jnp.where(sub >= at, tile, tiles[t + 1])
        return pltpu.roll(tile, (to - at) % SUB, 0) if (to - at) % SUB else tile

    for k, x, t, at in short_places(width, depth):
        blank = 1.0 if k == 6 else 0.0
        tile = jnp.where((sub < depth) & jnp.broadcast_to(has_after, (SUB, lanes)), short_rows(after, t, at, 0), blank)
        upper_rows = (sub >= SUB - depth) & jnp.broadcast_to(has_before, (SUB, lanes))
        ext[k, margin + x, rows:] = jnp.where(upper_rows, short_rows(before, t, at, SUB - depth), tile)
    for k in range(7):
        for x in range(width if k in LONG else 0):
            j, upper = x % (width // 2), x // (width // 2)
            tile = tail_tile(low, odd, *from_sides(LONG.index(k) * (width // 2) + j), upper)
            ext[k, margin + x, rows:] = jnp.where(valid, tile, 0.0)
    at = 0
    for k, depth in enumerate(depths(margin)):
        for j in range(depth):
            outer[at + j] = ext[k, margin + core * (width - depth) + j, rows:]
        at += depth


def join_inner(margin, count_y, ext_in, ext, inner):
    del ext_in
    width, rows, lanes = ext.shape[1] - 2 * margin, ext.shape[2] - SUB, ext.shape[3]
    _, at_y, core, _ = position()
    valid = valid_rows(low_half(lanes), at_y, count_y)
    at = 0
    for k, depth in enumerate(depths(margin)):
        for j in range(depth):
            inner[at + j] = ext[k, margin + (1 - core) * (width - depth) + j, rows:]
        at += depth
    scale = COURANT * COURANT
    for x in range(margin, margin + width):
        ext[6, x, 0:rows] = scale / ext[6, x, 0:rows]
        ext[6, x, rows:] = jnp.where(valid, scale / ext[6, x, rows:], 0.0)


def load_rest(ext_in, forward, mask, offsets, taps, ext, forward_out, mask_out, weights, table, sems):
    del ext_in, ext
    lists = [pltpu.make_async_copy(offsets, table[0], sems.at[0]), pltpu.make_async_copy(taps, table[1], sems.at[1])]
    loads = [pltpu.make_async_copy(forward, forward_out, sems.at[2]), pltpu.make_async_copy(mask, mask_out, sems.at[3])]
    for load in lists + loads:
        load.start()
    for load in lists:
        load.wait()
    distance = lax.broadcasted_iota(jnp.int32, weights.shape, 0) - weights.shape[0] // 2
    total = jnp.zeros(weights.shape, jnp.float32)
    for b in range(offsets.shape[0]):
        total = total + jnp.where(distance == table[0][b], table[1][b], 0.0)
    weights[...] = total
    for load in loads:
        load.wait()


def join_core(margin, ext_in, in_x, ext):
    del ext_in
    width, rows = ext.shape[1] - 2 * margin, ext.shape[2] - SUB
    _, _, core, _ = position()
    in_at = (1 - core) * (width + margin)
    at = 0
    for k, depth in enumerate(depths(margin)):
        for j in range(depth):
            plane = in_x[at + j]
            plane = COURANT * COURANT / plane if k == 6 else plane
            ext[k, in_at + core * (margin - depth) + j, 0:rows] = plane
        at += depth


def join_outer(margin, count_x, ext_in, out_x, ext):
    del ext_in
    width, rows = ext.shape[1] - 2 * margin, ext.shape[2] - SUB
    at_x, _, core, _ = position()
    has_out = has_outward(at_x, core, count_x)
    out_at = core * (width + margin)
    at = 0
    for k, depth in enumerate(depths(margin)):
        for j in range(depth):
            plane = out_x[at + j]
            plane = COURANT * COURANT / plane if k == 6 else plane
            ext[k, out_at + (1 - core) * (margin - depth) + j, 0:rows] = jnp.where(has_out, plane, 0.0)
        at += depth


def join_corner(margin, count_x, count_y, ext_in, outer, ext):
    del ext_in
    width, rows, lanes = ext.shape[1] - 2 * margin, ext.shape[2] - SUB, ext.shape[3]
    at_x, at_y, core, _ = position()
    has_out = has_outward(at_x, core, count_x)
    valid = valid_rows(low_half(lanes), at_y, count_y) & jnp.broadcast_to(has_out, (SUB, lanes))
    out_at = core * (width + margin)
    at = 0
    for k, depth in enumerate(depths(margin)):
        for j in range(depth):
            tile = outer[at + j]
            tile = jnp.where(valid, COURANT * COURANT / tile, 0.0) if k == 6 else jnp.where(has_out, tile, 0.0)
            ext[k, out_at + (1 - core) * (margin - depth) + j, rows:] = tile
        at += depth


def steps(margin, ranges, product, ext, forward, mask, masked, final):
    width, rows, lanes = mask.shape
    high = rows + SUB
    at_x, at_y, _, _ = position()
    low = low_half(lanes)
    lane = lax.broadcasted_iota(jnp.int32, (high, lanes), 1)
    first_lane, last_lane = lane == 0, lane == lanes - 1
    before_rows = jnp.where(low | jnp.broadcast_to(at_y > 0, (SUB, lanes)), 1.0, 0.0)
    before_x = jnp.where(at_x > 0, 1.0, 0.0)

    gap = lax.broadcasted_iota(jnp.int32, (lanes, lanes), 0) - lax.broadcasted_iota(jnp.int32, (lanes, lanes), 1)
    ahead = jnp.where(gap == 1, 1.0, 0.0) - jnp.where(gap == 0, 1.0, 0.0)
    ahead = jnp.concatenate([ahead, ahead], 0).astype(jnp.bfloat16)

    def ahead_z(first, end):
        f = ext[0:2, first:end].reshape(2 * (end - first) * high, lanes)
        main = f.astype(jnp.bfloat16)
        rest = (f - main.astype(jnp.float32)).astype(jnp.bfloat16)
        return jnp.dot(jnp.concatenate([main, rest], 1), ahead, preferred_element_type=jnp.float32)

    def next_y(f):
        return pltpu.roll(f, high - 1, 0)

    def last_y(f):
        return pltpu.roll(f, 1, 0)

    def next_z(f):
        return jnp.where(last_lane, 0.0, pltpu.roll(f, lanes - 1, 1))

    def last_z(f):
        return jnp.where(first_lane, 0.0, pltpu.roll(f, 1, 1))

    for turn, (first, first_e, end_h, end_e) in enumerate(ranges):
        last = turn == margin - 1
        if product:
            both = ahead_z(first, end_h)
        held_y = held_z = None
        for i in range(first, end_e):
            ex, ey, ez = ext[0, i], ext[1, i], ext[2, i]
            hx, hy, hz = ext[3, i], ext[4, i], ext[5, i]
            if i < end_h:
                ey_x, ez_x = ext[1, i + 1], ext[2, i + 1]
                if turn == 0:
                    hx, hy, hz = hx * (1 / COURANT), hy * (1 / COURANT), hz * (1 / COURANT)
                if product:
                    ahead_x, ahead_y = (both[n * high : (n + 1) * high] for n in (i - first, i - first + end_h - first))
                else:
                    ahead_x, ahead_y = next_z(ex) - ex, next_z(ey) - ey
                hx = hx - ((next_y(ez) - ez) - ahead_y)
                hy = hy - (ahead_x - (ez_x - ez))
                hz = hz - ((ey_x - ey) - (next_y(ex) - ex))

                def clear(h):
                    h = jnp.concatenate([h[:rows], h[rows:] * before_rows], 0)
                    return h * before_x if i < margin else h

                hx, hy, hz = clear(hx), clear(hy), clear(hz)
                ext[3, i], ext[4, i], ext[5, i] = hx, hy, hz
            if i >= first_e:
                if held_y is None:
                    held_y, held_z = ext[4, i - 1], ext[5, i - 1]
                c = ext[6, i]
                ex = ex + c * ((hz - last_y(hz)) - (hy - last_z(hy)))
                ey = ey + c * ((hx - last_z(hx)) - (hz - held_z))
                ez = ez + c * ((hy - held_y) - (hx - last_y(hx)))
                if not last:
                    ext[0, i], ext[1, i], ext[2, i] = ex, ey, ez
                if margin <= i < margin + width:
                    x = i - margin
                    own_e = (ex[:rows], ey[:rows], ez[:rows])
                    total = sum(forward[turn, a, x].astype(jnp.float32) * own_e[a] for a in range(3))
                    if turn > 0:
                        total = total + masked[x]
                    if last:
                        total = total * mask[x].astype(jnp.float32)
                        for a in range(3):
                            final[a, x] = own_e[a]
                    masked[x] = total
            held_y, held_z = hy, hz


def inner_ranges(margin, width, core):
    top = width + 2 * margin - 1
    if core == 1:
        return [(t, t + 1, top - margin - t, top - margin - t) for t in range(margin)]
    return [(margin + t, margin + t + 1, top - t, top - t) for t in range(margin)]


def outer_ranges(margin, width, core):
    top = width + 2 * margin - 1
    if core == 1:
        return [(top - margin - t, top - margin - t, top - t, top - t) for t in range(margin)]
    return [(t, t + 1, margin + t, margin + t + 1) for t in range(margin)]


def early_steps(margin, count_y, ext_in, forward, mask, inner, ext, masked, final):
    del ext_in
    width, lanes = mask.shape[0], mask.shape[2]
    rows = mask.shape[1]
    _, at_y, core, _ = position()
    valid = valid_rows(low_half(lanes), at_y, count_y)
    in_at = (1 - core) * (width + margin)
    at = 0
    for k, depth in enumerate(depths(margin)):
        for j in range(depth):
            tile = inner[at + j]
            place = in_at + core * (margin - depth) + j
            ext[k, place, rows:] = jnp.where(valid, COURANT * COURANT / tile, 0.0) if k == 6 else tile
        at += depth
    for c in range(2):
        @pl.when(core == c)
        def _():
            steps(margin, inner_ranges(margin, width, c), True, ext, forward, mask, masked, final)


def late_steps(margin, reach, rounds, count_x, count_y, ext_in, masked_in, final_in, outer, forward, mask, weights, ext, masked, final, send):
    del masked_in, final_in
    _, _, core, _ = position()
    join_corner(margin, count_x, count_y, ext_in, outer, ext)
    for c in range(2):
        @pl.when(core == c)
        def _():
            steps(margin, outer_ranges(margin, mask.shape[0], c), False, ext, forward, mask, masked, final)
    band_hop(reach, rounds, None, 1, True, weights, masked, send)


def band_sum(reach, hop, sign, alone, weights, own, other, where, sums):
    width, _, lanes = own.shape
    _, _, core, _ = position()
    middle = weights.shape[0] // 2
    for j in range(width):
        for same in (True,) if alone else (True, False):
            plane = (own if same else other)[j, where]
            for x in range(width):
                distances = [j - x - 2 * hop * s * width + (0 if same else t * width) for s in (1, -1) for t in (1, -1)]
                if min(abs(distance) for distance in distances) > reach:
                    continue
                distance = j - x - 2 * hop * width * sign + (0 if same else (1 - 2 * core) * width)
                weight = jnp.broadcast_to(weights[pl.ds(middle + distance, 1)], (SUB, lanes))
                sums[x] = sums[x] + weight * plane
    return sums


def arrived(count_x, via_1, via_0, x, where):
    at_x, _, core, _ = position()
    first, second = via_1[x, where], via_0[x, where]
    up = core == 1
    before = jnp.where(at_x >= 2, jnp.where(up, first, second), 0.0)
    after = jnp.where(at_x < count_x - 2, jnp.where(up, second, first), 0.0)
    return before, after


def band_hop(reach, hop, count_x, up, alone, weights, own, *refs):
    *refs, send = refs
    other, via = (own, refs) if alone else (refs[0], refs[1:])
    width, rows, lanes = own.shape
    _, _, core, _ = position()
    ahead = core == up
    for r in range(rows // SUB):
        where = slice(r * SUB, (r + 1) * SUB)
        if via:
            start = [jnp.where(ahead, *arrived(count_x, *via, x, where)) for x in range(width)]
        else:
            start = [jnp.zeros((SUB, lanes), jnp.float32)] * width
        sums = band_sum(reach, hop, jnp.where(ahead, 1, -1), alone, weights, own, other, where, start)
        for x in range(width):
            send[x, where] = sums[x]


def band_own(reach, weights, own, other, final, base, stored, sem):
    store = pltpu.make_async_copy(final, stored, sem)
    store.start()
    width, rows, lanes = own.shape
    for r in range(rows // SUB):
        where = slice(r * SUB, (r + 1) * SUB)
        sums = band_sum(reach, 0, 1, False, weights, own, other, where, [jnp.zeros((SUB, lanes), jnp.float32)] * width)
        for x in range(width):
            base[x, where] = sums[x]
    store.wait()


def band_end(count_x, base, via_1, via_0, out):
    for x in range(out.shape[0]):
        before, after = arrived(count_x, via_1, via_0, x, slice(None))
        out[x] = base[x] + before + after


def shards(routes, adjoint_fields, forward_e, permittivity, design_mask, band_offsets, filter_taps):
    width, rows, lanes = permittivity.shape
    margin = ITERS
    f32 = jnp.float32
    planes = sum(depths(margin))
    shape = jax.ShapeDtypeStruct
    vmem = pl.BlockSpec(memory_space=pltpu.VMEM)
    hbm = pl.BlockSpec(memory_space=pltpu.HBM)
    params = pltpu.CompilerParams(vmem_limit_bytes=24 * 1024 * 1024)
    block = shape((width, rows, lanes), f32)
    ext = shape((7, width + 2 * margin, rows + SUB, lanes), f32)
    strip = shape((planes, rows, lanes), f32)
    edge = shape((sum(side_tiles(width, margin)), SUB, lanes), f32)
    corner = shape((planes, SUB, lanes), f32)
    reach = width * routes.count_x // 4
    rounds = -(-reach // (2 * width))
    distances = shape((4 * (rounds + 1) * width, lanes), f32)

    def cost(microseconds):
        return pl.CostEstimate(flops=int(microseconds * 1e9), bytes_accessed=int(microseconds * 3.6e6), transcendentals=0)

    def move(value, pairs):
        return lax.ppermute(value, BOTH, pairs)

    def from_hbm(*values):
        return [pltpu.with_memory_space_constraint(value, pltpu.HBM) for value in values]

    cells, side_a0, side_b, side_a1 = pl.pallas_call(
        functools.partial(pack_y, margin),
        out_shape=(ext, edge, edge, edge),
        in_specs=[hbm] * 2,
        out_specs=(vmem,) * 4,
        scratch_shapes=[pltpu.SemaphoreType.DMA((7,))],
        compiler_params=params,
        name="pack_y",
    )(*from_hbm(adjoint_fields, permittivity))
    out_x, in_x = pl.pallas_call(
        functools.partial(pack_x, margin),
        out_shape=(strip, strip),
        in_specs=[vmem],
        out_specs=(vmem,) * 2,
        compiler_params=params,
        name="pack_x",
    )(cells)
    side_a0 = move(side_a0, routes.side_a[0])
    side_b = move(side_b, routes.side_b)
    side_a1 = move(side_a1, routes.side_a[1])
    in_x = move(in_x, routes.core)
    out_x = move(out_x, routes.out_x)
    cells, forward_e, design_mask, weights = pl.pallas_call(
        load_rest,
        out_shape=(ext, pltpu.VMEM(forward_e.shape, forward_e.dtype), pltpu.VMEM(design_mask.shape, design_mask.dtype), distances),
        in_specs=[vmem] + [hbm] * 4,
        out_specs=(vmem,) * 4,
        input_output_aliases={0: 0},
        scratch_shapes=[
            (pltpu.SMEM(band_offsets.shape, band_offsets.dtype), pltpu.SMEM(filter_taps.shape, filter_taps.dtype)),
            pltpu.SemaphoreType.DMA((4,)),
        ],
        compiler_params=params,
        cost_estimate=cost(JOIN_X_US),
        name="load_rest",
    )(cells, *from_hbm(forward_e, design_mask, band_offsets, filter_taps))
    cells, outer = pl.pallas_call(
        functools.partial(join_y, margin, routes.count_y),
        out_shape=(ext, corner),
        in_specs=[vmem] * 4,
        out_specs=(vmem,) * 2,
        input_output_aliases={0: 0},
        compiler_params=params,
        cost_estimate=cost(JOIN_Y_US),
        name="join_y",
    )(cells, side_a0, side_b, side_a1)
    outer = move(outer, routes.out_x)
    cells, inner = pl.pallas_call(
        functools.partial(join_inner, margin, routes.count_y),
        out_shape=(ext, corner),
        in_specs=[vmem],
        out_specs=(vmem,) * 2,
        input_output_aliases={0: 0},
        compiler_params=params,
        cost_estimate=cost(JOIN_X_US),
        name="join_inner",
    )(cells)
    inner = move(inner, routes.core)
    cells = pl.pallas_call(
        functools.partial(join_core, margin),
        out_shape=ext,
        in_specs=[vmem] * 2,
        out_specs=vmem,
        input_output_aliases={0: 0},
        compiler_params=params,
        cost_estimate=cost(JOIN_X_US),
        name="join_core",
    )(cells, in_x)
    fields = pltpu.VMEM((3, width, rows, lanes), f32)
    cells, masked, final = pl.pallas_call(
        functools.partial(early_steps, margin, routes.count_y),
        out_shape=(ext, block, fields),
        in_specs=[vmem] * 4,
        out_specs=(vmem,) * 3,
        input_output_aliases={0: 0},
        compiler_params=params,
        cost_estimate=cost(JOIN_X_US),
        name="early_steps",
    )(cells, forward_e, design_mask, inner)
    cells = pl.pallas_call(
        functools.partial(join_outer, margin, routes.count_x),
        out_shape=ext,
        in_specs=[vmem] * 2,
        out_specs=vmem,
        input_output_aliases={0: 0},
        compiler_params=params,
        cost_estimate=cost(JOIN_X_US),
        name="join_outer",
    )(cells, out_x)
    _, masked, final, send_1 = pl.pallas_call(
        functools.partial(late_steps, margin, reach, rounds, routes.count_x, routes.count_y),
        out_shape=(ext, block, fields, block),
        in_specs=[vmem] * 7,
        out_specs=(vmem,) * 4,
        input_output_aliases={0: 0, 1: 1, 2: 2},
        compiler_params=params,
        cost_estimate=cost(JOIN_X_US),
        name="late_steps",
    )(cells, masked, final, outer, forward_e, design_mask, weights)

    other = move(masked, routes.core)
    via = []

    def hop_kernel(hop, up, alone):
        operands = [weights, masked] + ([] if alone else [other]) + via
        return pl.pallas_call(
            functools.partial(band_hop, reach, hop, routes.count_x, up, alone),
            out_shape=block,
            in_specs=[vmem] * len(operands),
            out_specs=vmem,
            compiler_params=params,
            name="band_hop",
        )(*operands)

    for hop in range(rounds, 0, -1):
        if hop < rounds:
            send_1 = hop_kernel(hop, 1, False)
        send_0 = hop_kernel(hop, 0, False)
        via = [move(send_1, routes.ring_1), move(send_0, routes.ring_0)]
    base, final = pl.pallas_call(
        functools.partial(band_own, reach),
        out_shape=(block, shape(final.shape, f32)),
        in_specs=[vmem] * 4,
        out_specs=(vmem, hbm),
        scratch_shapes=[pltpu.SemaphoreType.DMA],
        compiler_params=params,
        cost_estimate=cost(BAND_OWN_US),
        name="band_own",
    )(weights, masked, other, final)
    filtered = pl.pallas_call(
        functools.partial(band_end, routes.count_x),
        out_shape=block,
        in_specs=[vmem] * 3,
        out_specs=vmem,
        compiler_params=params,
        name="band_end",
    )(base, *via)
    return filtered, final


def solution(mesh):
    routes = Routes(mesh.shape["gx"], mesh.shape["gy"])
    return jax.shard_map(
        functools.partial(shards, routes),
        mesh=mesh,
        in_specs=(
            P(None, "gx", "gy", None),
            P(None, None, "gx", "gy", None),
            P("gx", "gy", None),
            P("gx", "gy", None),
            P(),
            P(),
        ),
        out_specs=(P("gx", "gy", None), P(None, "gx", "gy", None)),
        check_vma=False,
    )
```
